128 devices in a mesh: dp: 16 (over z, x), seq: 8 (over y, core).
Axes of the slice: x: 4, y: 4, z: 4, core: 2. Of those that a mesh axis runs over, the one named last changes fastest.
Arguments:
- hidden: bfloat16 [16, 2, 1024, 5120], P('dp', None, 'seq'), may hold values from -6 to 6
- frozen_queries: bfloat16 [16, 2, 1024, 8192], P('dp', None, 'seq'), may hold values from -120 to 120
- frozen_keys: bfloat16 [16, 2, 1024, 1024], P('dp', None, 'seq'), may hold values from -5 to 5
- frozen_value_matrix: bfloat16 [16, 2, 1024, 1024], P('dp', None, 'seq'), may hold values from -6 to 6
- response_index: int32 [16, 2, 1024], P('dp'), may hold values from 0 to 2, never falling along the last dimension, each value on 1 to 512 neighbouring positions
- partner: int32 [16], P('dp'), may hold values from 0 to 15, as said below
- adapter_down_weight: bfloat16 [5120, 64], replicated, may hold values from -0.078125 to 0.078125
- adapter_up_weight: bfloat16 [64, 1024], replicated, may hold values from -0.75 to 0.75
Outputs:
- attention_out: bfloat16 [16, 2, 1024, 8192], P('dp', None, 'seq')
The draws below stay inside these ranges and needn't reach their ends.
Inputs may be any that keep to these rules, and one draw needn't show every extreme that they name: partner[r] = r XOR m for one m with 1 <= m < 16, the same for every rank.
All inputs are finite; a program needn't handle non-finite values.
Results may differ from the reference program's by a relative error of at most 0.011.
Values may be sent and summed in bfloat16 or wider, within the bound.
No kernel may reach another device: no remote copies, remote signals or barrier semaphores. Data moves between devices by JAX's collectives and lax.ppermute only.
A program may use at most 128 MiB of HBM per device.

```python
import math
import jax
import jax.numpy as jnp
import numpy as np
from jax import lax

MODEL_WIDTH = 5120
HEADS = 64
KEY_VALUE_HEADS = 8
HEAD_SIZE = 128
ADAPTER_RANK = 64
SEGS = 3
RANKS = 16
HALF = 1024


def shared_keys(key, blend):
    rows = jnp.clip(jax.random.normal(key, (RANKS, 2, HALF, KEY_VALUE_HEADS * HEAD_SIZE), jnp.float32), -5.0, 5.0)
    places = jnp.arange(HALF)
    aligned = places % 61 == 30
    following = jnp.roll(aligned, -1).astype(jnp.float32)
    mixing = (blend * following)[:, None]
    rows = rows * (1.0 - mixing)
    return rows


def draw_frozen_keys(key, part):
    rows = shared_keys(key, 0.0)
    return rows.astype(jnp.bfloat16)


def draw_frozen_queries(key, part):
    own_key = jax.random.fold_in(key, 11)
    shape = (RANKS, 2, HALF, HEADS * HEAD_SIZE)
    rows = jnp.clip(jax.random.normal(own_key, shape, jnp.float32), -5.0, 5.0)
    return rows.astype(jnp.bfloat16)


def draw_partner(key, part):
    key = jax.random.fold_in(key, 23)
    words = jax.random.randint(key, (2,), 0, 1000003, dtype=jnp.int32)
    mixed = (words[0] * 7919 + words[1]) % 1000003
    offset = (mixed % (RANKS - 1) + 1).astype(jnp.int32)
    return jnp.bitwise_xor(jnp.arange(RANKS, dtype=jnp.int32), offset)


def steps_of(key, shape, split, least, high):
    factor_of, own = 1.0, jax.random.fold_in(key, 6)
    for axis_at, parts in split:
        steps = jnp.exp(jax.random.uniform(jax.random.fold_in(own, axis_at), (parts,), jnp.float32, least / len(split), high / len(split)))
        factor_of = factor_of * jnp.repeat(steps, shape[axis_at] // parts).reshape([-1 if axis == axis_at else 1 for axis in range(len(shape))])
    return factor_of


def profile(amount, total, reach, lean):
    portions = [(1 << 20) // math.isqrt(rank ** lean) + 1 for rank in range(2, amount + 1)]
    spare, counts = total - reach - (amount - 1), [1] * (amount - 1)
    while spare > 0:
        movable = [i for i in range(amount - 1) if counts[i] < reach]
        mass, budget = sum([portions[i] for i in movable]), spare
        for i in movable:
            extra = min(reach - counts[i], max(1, budget * portions[i] // mass), spare)
            counts[i] = counts[i] + extra
            spare = spare - extra
    return np.array([reach] + counts)


def uneven(key, count, total, bound, skew):
    if count == 2:
        one = jax.random.randint(key, (), max(1, total - bound), min(bound, total - 1) + 1)
        return jnp.stack([one, total - one])
    tallies = jnp.asarray(profile(count, total, bound, skew), jnp.int32)
    pairs = (count - 1) // 2
    donor, receiver = tallies[1:1 + 2 * pairs:2], tallies[2:2 + 2 * pairs:2]
    slack = jnp.minimum(donor - 1, bound - receiver)
    shifted = jax.random.randint(jax.random.fold_in(key, 1), (pairs,), 0, 1 << 20) % (slack + 1)
    tallies = tallies.at[1:1 + 2 * pairs:2].set(donor - shifted).at[2:2 + 2 * pairs:2].set(receiver + shifted)
    return tallies[jax.random.permutation(jax.random.fold_in(key, 2), count)]


def bell_draw(key, dims, spread, most, shards=(), kind=jnp.bfloat16):
    drawn = jax.random.normal(key, dims, jnp.float32) * spread
    if len(shards) > 0:
        drawn = steps_of(key, dims, shards, -0.22, 0.18) * drawn
    return jnp.clip(drawn, min=-most, max=most).astype(kind)


def setup_inputs(seed: int = 0) -> dict:
    streams_of = jax.random.split(jax.random.key(seed), 9)
    hidden = bell_draw(streams_of[0], (RANKS, 2, HALF, MODEL_WIDTH), 1.0, 6.0, ((0, 16), (2, 8)))
    frozen_queries = draw_frozen_queries(jax.random.fold_in(streams_of[8], 71), 0)
    frozen_keys = draw_frozen_keys(jax.random.fold_in(streams_of[8], 71), 0)
    frozen_value_matrix = bell_draw(streams_of[3], (RANKS, 2, HALF, KEY_VALUE_HEADS * HEAD_SIZE), 1.0, 6.0, ((0, 16), (2, 8)))
    response_index = jax.vmap(lambda own: jnp.searchsorted(jnp.cumsum(uneven(own, SEGS, HALF, HALF // 2, 2)), jnp.arange(HALF), side="right"))(jax.random.split(streams_of[4], RANKS * 2)).reshape((RANKS, 2, HALF)).astype(jnp.int32)
    partner = draw_partner(jax.random.fold_in(streams_of[8], 71), 0)
    adapter_down_weight = bell_draw(streams_of[6], (MODEL_WIDTH, ADAPTER_RANK), MODEL_WIDTH ** -0.5, 0.078125)
    adapter_up_weight = bell_draw(streams_of[7], (ADAPTER_RANK, KEY_VALUE_HEADS * HEAD_SIZE), ADAPTER_RANK ** -0.5, 0.75)
    return {"hidden": hidden, "frozen_queries": frozen_queries, "frozen_keys": frozen_keys, "frozen_value_matrix": frozen_value_matrix, "response_index": response_index, "partner": partner, "adapter_down_weight": adapter_down_weight, "adapter_up_weight": adapter_up_weight}


ADAPTER_SCALE = 2.0


def attend(queries, key_rows, value_row_block, query_labels, key_labels, query_places, key_places):
    kv_heads = key_rows.shape[1] // HEAD_SIZE
    group_size = queries.shape[1] // (kv_heads * HEAD_SIZE)
    allowed = (query_labels[:, None] == key_labels[None, :]) & (key_places[None, :] <= query_places[:, None])

    def one_group(head_group):
        offset = head_group * group_size * HEAD_SIZE
        query_block = lax.dynamic_slice_in_dim(queries, offset, group_size * HEAD_SIZE, 1)
        query_block = query_block.reshape(queries.shape[0], group_size, HEAD_SIZE)
        key_block = lax.dynamic_slice_in_dim(key_rows, head_group * HEAD_SIZE, HEAD_SIZE, 1)
        value_block = lax.dynamic_slice_in_dim(value_row_block, head_group * HEAD_SIZE, HEAD_SIZE, 1)
        scores = jnp.einsum("rgd,cd->rgc", query_block.astype(jnp.float32), key_block.astype(jnp.float32))
        scores = scores * (1.0 / HEAD_SIZE ** 0.5)
        scores = jnp.where(allowed[:, None, :], scores, -jnp.inf)
        row_max = jnp.max(scores, axis=2, keepdims=True)
        raised = jnp.exp(scores - row_max)
        weights = (raised / jnp.sum(raised, axis=2, keepdims=True)).astype(jnp.bfloat16)
        blended = jnp.einsum("rgc,cd->rgd", weights.astype(jnp.float32), value_block.astype(jnp.float32))
        return blended.astype(jnp.bfloat16)

    blocks = lax.map(one_group, jnp.arange(kv_heads, dtype=jnp.int32))
    return jnp.transpose(blocks, (1, 0, 2, 3)).reshape(queries.shape[0], queries.shape[1])


def reference(hidden, frozen_queries, frozen_keys, frozen_value_matrix, response_index, partner, adapter_down_weight, adapter_up_weight):
    reduced_state = jnp.dot(hidden, adapter_down_weight, preferred_element_type=jnp.float32).astype(jnp.bfloat16)
    value_matrix = (frozen_value_matrix.astype(jnp.float32) + ADAPTER_SCALE * jnp.dot(reduced_state, adapter_up_weight, preferred_element_type=jnp.float32)).astype(jnp.bfloat16)
    places = jnp.arange(HALF, dtype=jnp.int32)

    def one_item(item_index):
        rank_index = item_index // 2
        half_index = item_index % 2
        source = jnp.where(half_index == 0, rank_index, partner[rank_index]).astype(jnp.int32)

        def select(whole):
            picked = lax.dynamic_index_in_dim(whole, source, 0, False)
            return lax.dynamic_index_in_dim(picked, half_index.astype(jnp.int32), 0, False)

        labels = select(response_index)
        return attend(select(frozen_queries), select(frozen_keys), select(value_matrix), labels, labels, places, places)

    outputs = lax.map(one_item, jnp.arange(2 * RANKS, dtype=jnp.int32))
    return outputs.reshape(RANKS, 2, HALF, HEADS * HEAD_SIZE)
```

```python
import functools

import jax
import jax.numpy as jnp
from jax import lax
from jax.experimental import pallas as pl
from jax.experimental.pallas import tpu as pltpu
from jax.sharding import PartitionSpec as P

HEAD = 128
GROUP = 8
KV = 8
ROWS = 128
SPAN = GROUP * HEAD
PAIR = 2
ADAPTER_SCALE = 2.0
EXP2_SCALE = 1.4426950408889634 / HEAD**0.5
MASKED = -jnp.inf
VMEM_LIMIT = 60 << 20

KEPT = 4
MOVED = KV - KEPT
LABELS_AT = MOVED * 2 * HEAD


def fill_bias(bias_ref, own_at, places, label_at):
    def label_row(at):
        found = jnp.where(at >= 0, label_at(jnp.maximum(at, 0)).astype(jnp.float32), -1.0)
        return jnp.broadcast_to(found, (ROWS, ROWS))

    mine = label_row(own_at)
    query_label = mine.T
    merged = jnp.where(causal(), mine, label_row(own_at - 4))
    for at, tile in enumerate([merged] + [label_row(place) for place in places]):
        bias_ref[at] = jnp.where(tile == query_label, 0.0, MASKED)


def other_places(own_at):
    low_core = lax.rem(own_at, 2) == 0
    return own_at - 2, jnp.where(low_core, own_at - 1, own_at - 3), jnp.where(low_core, own_at - 3, own_at - 1)


def causal():
    rows = lax.broadcasted_iota(jnp.int32, (ROWS, ROWS), 0)
    return lax.broadcasted_iota(jnp.int32, (ROWS, ROWS), 1) <= rows


def adapter_kernel(
    place_ref, labels_ref, hidden_ref, down_ref, frozen_ref, key_ref, up_ref, query_ref,
    near_ref, moved_ref, moved_query_ref, bias_zero_ref, bias_one_ref, low_ref, sem,
):
    step = pl.program_id(0)
    copy = pltpu.make_async_copy(query_ref.at[0, 1, :, pl.ds(KEPT * SPAN, MOVED * SPAN)], moved_query_ref, sem)

    @pl.when(step == 0)
    def _():
        copy.start()
        low_ref[...] = jnp.zeros_like(low_ref)
        own_at = place_ref[0]
        for half, bias_ref in enumerate((bias_zero_ref, bias_one_ref)):
            label_at = lambda at: labels_ref[half : half + 1, pl.ds(pl.multiple_of(at * ROWS, ROWS), ROWS)]
            fill_bias(bias_ref, own_at, other_places(own_at), label_at)

    low_ref[...] += lax.dot_general(
        hidden_ref[...].reshape(2 * ROWS, hidden_ref.shape[-1]),
        down_ref[...],
        (((1,), (1,)), ((), ())),
        preferred_element_type=jnp.float32,
    )

    @pl.when(step == pl.num_programs(0) - 1)
    def _():
        low = low_ref[...].astype(jnp.bfloat16)
        delta = jnp.dot(low, up_ref[...], preferred_element_type=jnp.float32)
        for half in range(2):
            own = delta[half * ROWS : (half + 1) * ROWS]
            values = (frozen_ref[half].astype(jnp.float32) + ADAPTER_SCALE * own).astype(jnp.bfloat16)
            for head in range(KV):
                if half == 0:
                    out, at = near_ref, KEPT + head
                else:
                    out, at = (near_ref, head) if head < KEPT else (moved_ref, head - KEPT)
                cols = slice(head * HEAD, (head + 1) * HEAD)
                out[:, 2 * at * HEAD : (2 * at + 1) * HEAD] = key_ref[half, :, cols]
                out[:, (2 * at + 1) * HEAD : (2 * at + 2) * HEAD] = values[:, cols]
        labels = [labels_ref[1:2, at * ROWS : (at + 1) * ROWS].astype(jnp.float32) for at in range(8)]
        labels = jnp.concatenate(labels + [jnp.zeros((ROWS - 8, HEAD), jnp.float32)], axis=0)
        moved_ref[:, LABELS_AT:] = labels.astype(jnp.bfloat16)
        copy.wait()


def adapter(place, labels, hidden, frozen_values, keys, down, up, queries):
    width = hidden.shape[-1]
    steps = 4
    part = width // steps
    rank = down.shape[0]
    shapes = [
        ((ROWS, (KEPT + KV) * 2 * HEAD), jnp.bfloat16),
        ((ROWS, LABELS_AT + HEAD), jnp.bfloat16),
        ((ROWS, MOVED * SPAN), jnp.bfloat16),
        ((4, ROWS, ROWS), jnp.float32),
        ((4, ROWS, ROWS), jnp.float32),
    ]
    return pl.pallas_call(
        adapter_kernel,
        grid_spec=pltpu.PrefetchScalarGridSpec(
            num_scalar_prefetch=1,
            grid=(steps,),
            in_specs=[
                pl.BlockSpec((None, 2, 8 * ROWS), lambda i, p: (0, 0, 0)),
                pl.BlockSpec((None, 2, ROWS, part), lambda i, p: (0, 0, 0, i)),
                pl.BlockSpec((rank, part), lambda i, p: (0, i)),
                pl.BlockSpec((None, 2, ROWS, KV * HEAD), lambda i, p: (0, 0, 0, 0)),
                pl.BlockSpec((None, 2, ROWS, KV * HEAD), lambda i, p: (0, 0, 0, 0)),
                pl.BlockSpec((rank, KV * HEAD), lambda i, p: (0, 0)),
                pl.BlockSpec(memory_space=pl.ANY),
            ],
            out_specs=[
                pl.BlockSpec(memory_space=pl.ANY) if at == 2 else pl.BlockSpec(shape, lambda i, p, n=len(shape): (0,) * n)
                for at, (shape, _) in enumerate(shapes)
            ],
            scratch_shapes=[pltpu.VMEM((2 * ROWS, rank), jnp.float32), pltpu.SemaphoreType.DMA],
        ),
        out_shape=[jax.ShapeDtypeStruct(*shape) for shape in shapes],
        compiler_params=pltpu.CompilerParams(vmem_limit_bytes=60 << 20),
        cost_estimate=pl.CostEstimate(flops=1 << 20, bytes_accessed=1 << 20, transcendentals=0),
        name="adapter",
    )(place, labels, hidden, down, frozen_values, keys, up, queries)


def near_attention_kernel(unroll, bias_ref, query_ref, own_ref, far_ref, two_ref, x_ref, w_ref, out_ref, key_ref, value_ref):
    blocks = (own_ref, far_ref, two_ref, x_ref, w_ref)
    attend(unroll, bias_ref, query_ref, blocks, out_ref, key_ref, value_ref)


def moved_attention_kernel(
    unroll, place_ref, label_ref, query_ref, own_ref, far_ref, two_ref, x_ref, w_ref, _,
    out_ref, bias_ref, key_ref, value_ref,
):
    @pl.when(pl.program_id(0) == 0)
    def _():
        own_at = place_ref[0]
        rows = label_ref[...].astype(jnp.float32)
        chosen = lax.broadcasted_iota(jnp.int32, rows.shape, 0)

        def label_at(at):
            return jnp.sum(jnp.where(chosen == at, rows, 0.0), axis=0, keepdims=True)

        fill_bias(bias_ref, own_at, other_places(own_at), label_at)

    blocks = (own_ref, far_ref, two_ref, x_ref, w_ref)
    attend(unroll, bias_ref, query_ref, blocks, out_ref, key_ref, value_ref)


def attend(unroll, bias_ref, query_ref, blocks, out_ref, key_ref, value_ref):
    is_causal = causal()

    @pl.when(pl.program_id(0) == 0)
    def _():
        value_ref[:, HEAD:] = jnp.ones((5 * ROWS, HEAD), jnp.bfloat16)

    for at, block in enumerate(blocks):
        span = slice(at * ROWS, (at + 1) * ROWS)
        key_ref[span, :] = block[:, :HEAD]
        value_ref[span, :HEAD] = block[:, HEAD:]

    def some_heads(step, carry):
        spans = [pl.ds(pl.multiple_of((step * PAIR + i) * HEAD, HEAD), HEAD) for i in range(PAIR)]
        queries = jnp.concatenate([query_ref[:, span] for span in spans], axis=0)
        scores = lax.dot_general(
            queries, key_ref[...], (((1,), (1,)), ((), ())), preferred_element_type=jnp.float32
        )
        weights = []
        for i in range(PAIR):
            mine = scores[i * ROWS : (i + 1) * ROWS]
            tiles = [jnp.where(is_causal, mine[:, :ROWS], mine[:, ROWS : 2 * ROWS]) + bias_ref[0]]
            tiles += [mine[:, (t + 1) * ROWS : (t + 2) * ROWS] + bias_ref[t] for t in range(1, 4)]
            peak = jnp.maximum(jnp.maximum(tiles[0], tiles[1]), jnp.maximum(tiles[2], tiles[3]))
            peak = jnp.max(peak, axis=1, keepdims=True)
            raised = [jnp.exp2((tile - peak) * EXP2_SCALE) for tile in tiles]
            near = jnp.where(is_causal, raised[0], 0.0).astype(jnp.bfloat16)
            far = jnp.where(is_causal, 0.0, raised[0]).astype(jnp.bfloat16)
            weights.append(
                jnp.concatenate([near, far] + [r.astype(jnp.bfloat16) for r in raised[1:]], axis=1)
            )
        blended = jnp.dot(
            jnp.concatenate(weights, axis=0), value_ref[...], preferred_element_type=jnp.float32
        )
        result = (blended[:, :HEAD] / blended[:, HEAD:]).astype(jnp.bfloat16)
        for i, span in enumerate(spans):
            out_ref[:, span] = result[i * ROWS : (i + 1) * ROWS]
        return carry

    steps = GROUP // PAIR
    if unroll == steps:
        for step in range(steps):
            some_heads(step, 0)
    else:
        lax.fori_loop(0, steps, some_heads, 0, unroll=unroll)


SCRATCH = [pltpu.VMEM((5 * ROWS, HEAD), jnp.bfloat16), pltpu.VMEM((5 * ROWS, 2 * HEAD), jnp.bfloat16)]
OUT = jax.ShapeDtypeStruct((1, 2, ROWS, KV * SPAN), jnp.bfloat16)


def near_attention(unroll, half, count, first, bias, queries, blocks, out_shape, out_spec):
    own, far, two, pair = blocks
    block_spec = pl.BlockSpec((ROWS, 2 * HEAD), lambda i: (0, first + i))
    return pl.pallas_call(
        functools.partial(near_attention_kernel, unroll),
        grid=(count,),
        in_specs=[
            pl.BlockSpec((4, ROWS, ROWS), lambda i: (0, 0, 0)),
            pl.BlockSpec((None, None, ROWS, SPAN), lambda i: (0, half, 0, i)),
        ]
        + [block_spec] * 3
        + [pl.BlockSpec((ROWS, 2 * HEAD), lambda i, row=row: (row, i)) for row in range(2)],
        out_specs=out_spec,
        scratch_shapes=SCRATCH,
        out_shape=out_shape,
        compiler_params=pltpu.CompilerParams(vmem_limit_bytes=VMEM_LIMIT),
        cost_estimate=pl.CostEstimate(flops=1 << 20, bytes_accessed=1 << 20, transcendentals=0),
        name="near_attention",
    )(bias, queries, own, far, two, pair, pair)


def moved_attention(place, queries, blocks, into):
    own, far, two, pair = blocks
    block_spec = pl.BlockSpec((ROWS, 2 * HEAD), lambda i, p: (0, i))
    return pl.pallas_call(
        functools.partial(moved_attention_kernel, 4),
        grid_spec=pltpu.PrefetchScalarGridSpec(
            num_scalar_prefetch=1,
            grid=(MOVED,),
            in_specs=[
                pl.BlockSpec((16, HEAD), lambda i, p: (0, LABELS_AT // HEAD)),
                pl.BlockSpec((ROWS, SPAN), lambda i, p: (0, i)),
            ]
            + [block_spec] * 3
            + [pl.BlockSpec((ROWS, 2 * HEAD), lambda i, p, row=row: (row, i)) for row in range(2)]
            + [pl.BlockSpec(memory_space=pl.ANY)],
            out_specs=pl.BlockSpec((None, None, ROWS, SPAN), lambda i, p: (0, 1, 0, KEPT + i)),
            scratch_shapes=[pltpu.VMEM((4, ROWS, ROWS), jnp.float32)] + SCRATCH,
        ),
        out_shape=OUT,
        input_output_aliases={8: 0},
        compiler_params=pltpu.CompilerParams(vmem_limit_bytes=VMEM_LIMIT),
        cost_estimate=pl.CostEstimate(flops=1 << 20, bytes_accessed=1 << 20, transcendentals=0),
        name="moved_attention",
    )(place, own, queries, own, far, two, pair, pair, into)


def shift(block, step):
    return lax.ppermute(block, "seq", [(s, s + step) for s in range(8 - step)])


def other_core(block):
    return lax.ppermute(block, "seq", [(s, s ^ 1) for s in range(8)])


def exchange(block, far, two, low_core, cols):
    pair = jnp.concatenate([two[:, cols], jnp.where(low_core, block[:, cols], far[:, cols])], axis=0)
    return block, far, two, other_core(pair)


def body(hidden, queries, keys, frozen_values, labels, partner, down, up):
    place = lax.axis_index("seq").astype(jnp.int32)
    low_core = lax.rem(place, 2) == 0
    place = place.reshape((1,))
    mask = jnp.bitwise_xor(partner[0], lax.axis_index("dp"))
    near, kv_moved, moved_queries, bias_zero, bias_one = adapter(
        place, labels, hidden, frozen_values, keys, down.T, up, queries
    )
    near_two, near_far = shift(near, 2), shift(near, 4)

    def route(m):
        return [(r, r ^ m) for r in range(16)]

    def move(m, kv_moved, moved_queries):
        return lax.ppermute(kv_moved, "dp", route(m)), lax.ppermute(moved_queries, "dp", route(m))

    kv_moved, moved_queries = lax.switch(
        mask - 1, [functools.partial(move, m) for m in range(1, 16)], kv_moved, moved_queries
    )
    kv_moved, moved_queries, near_two, near_far = lax.optimization_barrier(
        (kv_moved, moved_queries, near_two, near_far)
    )
    split = KEPT * 2 * HEAD
    kept_blocks = exchange(near, near_far, near_two, low_core, slice(0, split))
    zero_blocks = exchange(near, near_far, near_two, low_core, slice(split, None))
    sent = near_attention(
        4, 1, KEPT, 0, bias_one, queries, kept_blocks,
        jax.ShapeDtypeStruct((ROWS, KEPT * SPAN), jnp.bfloat16), pl.BlockSpec((ROWS, SPAN), lambda i: (0, i)),
    )

    def send(m, sent, kv_moved, bias, queries, *blocks):
        came = lax.ppermute(sent, "dp", route(m))
        two, far = shift(kv_moved, 2), shift(kv_moved, 4)
        spec = pl.BlockSpec((None, None, ROWS, SPAN), lambda i: (0, 0, 0, i))
        return came, two, far, near_attention(2, 0, KV, KEPT, bias, queries, blocks, OUT, spec)

    came, two, far, out = lax.switch(
        mask - 1, [functools.partial(send, m) for m in range(1, 16)], sent, kv_moved, bias_zero, queries, *zero_blocks
    )
    moved_blocks = exchange(kv_moved, far, two, low_core, slice(0, LABELS_AT))
    out = lax.dynamic_update_slice(out, came[None, None], (0, 1, 0, 0))
    return moved_attention(place, moved_queries, moved_blocks, out)


def solution(mesh):
    in_specs = (
        P("dp", None, "seq", None),
        P("dp", None, "seq", None),
        P("dp", None, "seq", None),
        P("dp", None, "seq", None),
        P("dp", None, None),
        P("dp"),
        P(),
        P(),
    )
    out_specs = P("dp", None, "seq", None)
    return jax.shard_map(body, mesh=mesh, in_specs=in_specs, out_specs=out_specs, check_vma=False)
```

```python
import functools

import jax
import jax.numpy as jnp
from jax import lax
from jax.experimental import pallas as pl
from jax.experimental.pallas import tpu as pltpu
from jax.sharding import PartitionSpec as P

HEAD = 128
GROUP = 8
KV = 8
ROWS = 128
SPAN = GROUP * HEAD
PAIR = 2
ADAPTER_SCALE = 2.0
EXP2_SCALE = 1.4426950408889634 / HEAD**0.5
MASKED = -jnp.inf
VMEM_LIMIT = 60 << 20
SMALL_VMEM_LIMIT = 24 << 20

KEPT = KV // 2
MOVED = KV // 2
LABELS_AT = MOVED * SPAN


def fill_bias(bias_ref, own_at, places, label_at):
    def label_row(at):
        found = jnp.where(at >= 0, label_at(jnp.maximum(at, 0)).astype(jnp.float32), -1.0)
        return jnp.broadcast_to(found, (ROWS, ROWS))

    mine = label_row(own_at)
    query_label = mine.T
    merged = jnp.where(causal(), mine, label_row(own_at - 4))
    for at, tile in enumerate([merged] + [label_row(place) for place in places]):
        bias_ref[at] = jnp.where(tile == query_label, 0.0, MASKED)


def other_places(own_at):
    low_core = lax.rem(own_at, 2) == 0
    return own_at - 2, jnp.where(low_core, own_at - 1, own_at - 3), jnp.where(low_core, own_at - 3, own_at - 1)


def causal():
    rows = lax.broadcasted_iota(jnp.int32, (ROWS, ROWS), 0)
    return lax.broadcasted_iota(jnp.int32, (ROWS, ROWS), 1) <= rows


def adapter_kernel(
    place_ref, labels_ref, hidden_ref, down_ref, frozen_ref, key_ref, up_ref, first_query_ref, second_query_ref,
    near_ref, moved_ref, moved_query_ref, bias_zero_ref, bias_one_ref, low_ref,
):
    step = pl.program_id(0)
    for at, query_ref in enumerate((first_query_ref, second_query_ref)):
        moved_query_ref[:, pl.ds(pl.multiple_of((2 * step + at) * SPAN, SPAN), SPAN)] = query_ref[...]

    @pl.when(step == 0)
    def _():
        low_ref[...] = jnp.zeros_like(low_ref)
        own_at = place_ref[0]
        for half, bias_ref in enumerate((bias_zero_ref, bias_one_ref)):
            label_at = lambda at: labels_ref[half : half + 1, pl.ds(pl.multiple_of(at * ROWS, ROWS), ROWS)]
            fill_bias(bias_ref, own_at, other_places(own_at), label_at)

    low_ref[...] += lax.dot_general(
        hidden_ref[...].reshape(2 * ROWS, hidden_ref.shape[-1]),
        down_ref[...],
        (((1,), (1,)), ((), ())),
        preferred_element_type=jnp.float32,
    )

    @pl.when(step == pl.num_programs(0) - 1)
    def _():
        low = low_ref[...].astype(jnp.bfloat16)
        delta = jnp.dot(low, up_ref[...], preferred_element_type=jnp.float32)
        for half in range(2):
            own = delta[half * ROWS : (half + 1) * ROWS]
            values = (frozen_ref[half].astype(jnp.float32) + ADAPTER_SCALE * own).astype(jnp.bfloat16)
            for head in range(KV):
                if half == 0:
                    out, at = near_ref, KEPT + head
                else:
                    out, at = (moved_ref if head % 2 else near_ref), head // 2
                cols = slice(head * HEAD, (head + 1) * HEAD)
                out[:, 2 * at * HEAD : (2 * at + 1) * HEAD] = key_ref[half, :, cols]
                out[:, (2 * at + 1) * HEAD : (2 * at + 2) * HEAD] = values[:, cols]
        labels = [labels_ref[1:2, at * ROWS : (at + 1) * ROWS].astype(jnp.float32) for at in range(8)]
        labels = jnp.concatenate(labels + [jnp.zeros((ROWS - 8, HEAD), jnp.float32)], axis=0)
        moved_query_ref[:, LABELS_AT:] = labels.astype(jnp.bfloat16)


def adapter(place, labels, hidden, frozen_values, keys, down, up, queries):
    width = hidden.shape[-1]
    steps = MOVED // 2
    part = width // steps
    rank = down.shape[0]
    shapes = [
        ((ROWS, (KEPT + KV) * 2 * HEAD), jnp.bfloat16),
        ((ROWS, MOVED * 2 * HEAD), jnp.bfloat16),
        ((ROWS, LABELS_AT + HEAD), jnp.bfloat16),
        ((4, ROWS, ROWS), jnp.float32),
        ((4, ROWS, ROWS), jnp.float32),
    ]
    return pl.pallas_call(
        adapter_kernel,
        grid_spec=pltpu.PrefetchScalarGridSpec(
            num_scalar_prefetch=1,
            grid=(steps,),
            in_specs=[
                pl.BlockSpec((None, 2, 8 * ROWS), lambda i, p: (0, 0, 0)),
                pl.BlockSpec((None, 2, ROWS, part), lambda i, p: (0, 0, 0, i)),
                pl.BlockSpec((rank, part), lambda i, p: (0, i)),
                pl.BlockSpec((None, 2, ROWS, KV * HEAD), lambda i, p: (0, 0, 0, 0)),
                pl.BlockSpec((None, 2, ROWS, KV * HEAD), lambda i, p: (0, 0, 0, 0)),
                pl.BlockSpec((rank, KV * HEAD), lambda i, p: (0, 0)),
                pl.BlockSpec((None, None, ROWS, SPAN), lambda i, p: (0, 1, 0, 4 * i + 1)),
                pl.BlockSpec((None, None, ROWS, SPAN), lambda i, p: (0, 1, 0, 4 * i + 3)),
            ],
            out_specs=[pl.BlockSpec(shape, lambda i, p, n=len(shape): (0,) * n) for shape, _ in shapes],
            scratch_shapes=[pltpu.VMEM((2 * ROWS, rank), jnp.float32)],
        ),
        out_shape=[jax.ShapeDtypeStruct(*shape) for shape in shapes],
        compiler_params=pltpu.CompilerParams(vmem_limit_bytes=60 << 20),
        cost_estimate=pl.CostEstimate(flops=1 << 20, bytes_accessed=1 << 20, transcendentals=0),
        name="adapter",
    )(place, labels, hidden, down, frozen_values, keys, up, queries, queries)


def near_attention_kernel(unroll, bias_ref, query_ref, own_ref, far_ref, two_ref, pair_ref, out_ref, key_ref, value_ref):
    attend(unroll, bias_ref, query_ref, (own_ref, far_ref, two_ref, pair_ref), out_ref, 0, key_ref, value_ref)


def moved_attention_kernel(
    unroll, place_ref, label_ref, query_ref, own_ref, far_ref, two_ref, x_ref, w_ref, came_ref, _,
    out_ref, bias_ref, key_ref, value_ref,
):
    @pl.when(pl.program_id(0) == 0)
    def _():
        own_at = place_ref[0]
        rows = label_ref[...].astype(jnp.float32)
        chosen = lax.broadcasted_iota(jnp.int32, rows.shape, 0)

        def label_at(at):
            return jnp.sum(jnp.where(chosen == at, rows, 0.0), axis=0, keepdims=True)

        fill_bias(bias_ref, own_at, other_places(own_at), label_at)

    out_ref[:, :SPAN] = came_ref[...]
    attend(unroll, bias_ref, query_ref, (own_ref, far_ref, two_ref, x_ref, w_ref), out_ref, GROUP, key_ref, value_ref)


def attend(unroll, bias_ref, query_ref, blocks, out_ref, out_head, key_ref, value_ref):
    is_causal = causal()

    @pl.when(pl.program_id(0) == 0)
    def _():
        value_ref[:, HEAD:] = jnp.ones((5 * ROWS, HEAD), jnp.bfloat16)

    at = 0
    for block in blocks:
        span = slice(at, at + block.shape[0])
        key_ref[span, :] = block[:, :HEAD]
        value_ref[span, :HEAD] = block[:, HEAD:]
        at += block.shape[0]

    def some_heads(step, carry):
        spans = [pl.ds(pl.multiple_of((step * PAIR + i) * HEAD, HEAD), HEAD) for i in range(PAIR)]
        queries = jnp.concatenate([query_ref[:, span] for span in spans], axis=0)
        scores = lax.dot_general(
            queries, key_ref[...], (((1,), (1,)), ((), ())), preferred_element_type=jnp.float32
        )
        weights = []
        for i in range(PAIR):
            mine = scores[i * ROWS : (i + 1) * ROWS]
            tiles = [jnp.where(is_causal, mine[:, :ROWS], mine[:, ROWS : 2 * ROWS]) + bias_ref[0]]
            tiles += [mine[:, (t + 1) * ROWS : (t + 2) * ROWS] + bias_ref[t] for t in range(1, 4)]
            peak = jnp.maximum(jnp.maximum(tiles[0], tiles[1]), jnp.maximum(tiles[2], tiles[3]))
            peak = jnp.max(peak, axis=1, keepdims=True)
            raised = [jnp.exp2((tile - peak) * EXP2_SCALE) for tile in tiles]
            near = jnp.where(is_causal, raised[0], 0.0).astype(jnp.bfloat16)
            far = jnp.where(is_causal, 0.0, raised[0]).astype(jnp.bfloat16)
            weights.append(
                jnp.concatenate([near, far] + [r.astype(jnp.bfloat16) for r in raised[1:]], axis=1)
            )
        blended = jnp.dot(
            jnp.concatenate(weights, axis=0), value_ref[...], preferred_element_type=jnp.float32
        )
        result = (blended[:, :HEAD] / blended[:, HEAD:]).astype(jnp.bfloat16)
        for i in range(PAIR):
            span = pl.ds(pl.multiple_of((out_head + step * PAIR + i) * HEAD, HEAD), HEAD)
            out_ref[:, span] = result[i * ROWS : (i + 1) * ROWS]
        return carry

    steps = GROUP // PAIR
    if unroll == steps:
        for step in range(steps):
            some_heads(step, 0)
    else:
        lax.fori_loop(0, steps, some_heads, 0, unroll=unroll)


SCRATCH = [pltpu.VMEM((5 * ROWS, HEAD), jnp.bfloat16), pltpu.VMEM((5 * ROWS, 2 * HEAD), jnp.bfloat16)]
OUT = jax.ShapeDtypeStruct((1, 2, ROWS, KV * SPAN), jnp.bfloat16)


def block_specs(first):
    whole = pl.BlockSpec((ROWS, 2 * HEAD), lambda i, *p: (0, first + i))
    return [whole, whole, whole, pl.BlockSpec((2 * ROWS, 2 * HEAD), lambda i, *p: (0, i))]


def near_attention(vmem_limit, unroll, half, stride, count, first, bias, queries, blocks, out_shape, out_spec):
    return pl.pallas_call(
        functools.partial(near_attention_kernel, unroll),
        grid=(count,),
        in_specs=[
            pl.BlockSpec((4, ROWS, ROWS), lambda i: (0, 0, 0)),
            pl.BlockSpec((None, None, ROWS, SPAN), lambda i: (0, half, 0, stride * i)),
        ]
        + block_specs(first),
        out_specs=out_spec,
        scratch_shapes=SCRATCH,
        out_shape=out_shape,
        compiler_params=pltpu.CompilerParams(vmem_limit_bytes=vmem_limit),
        cost_estimate=pl.CostEstimate(flops=1 << 20, bytes_accessed=1 << 20, transcendentals=0),
        name="near_attention",
    )(bias, queries, *blocks)


def moved_attention(place, queries, blocks, came, into):
    return pl.pallas_call(
        functools.partial(moved_attention_kernel, 4),
        grid_spec=pltpu.PrefetchScalarGridSpec(
            num_scalar_prefetch=1,
            grid=(MOVED,),
            in_specs=[
                pl.BlockSpec((16, HEAD), lambda i, p: (0, LABELS_AT // HEAD)),
                pl.BlockSpec((ROWS, SPAN), lambda i, p: (0, i)),
            ]
            + [pl.BlockSpec((ROWS, 2 * HEAD), lambda i, p: (0, i))] * 5
            + [pl.BlockSpec((ROWS, SPAN), lambda i, p: (0, i)), pl.BlockSpec(memory_space=pl.ANY)],
            out_specs=pl.BlockSpec((None, None, ROWS, 2 * SPAN), lambda i, p: (0, 1, 0, i)),
            scratch_shapes=[pltpu.VMEM((4, ROWS, ROWS), jnp.float32)] + SCRATCH,
        ),
        out_shape=OUT,
        input_output_aliases={9: 0},
        compiler_params=pltpu.CompilerParams(vmem_limit_bytes=SMALL_VMEM_LIMIT),
        cost_estimate=pl.CostEstimate(flops=1 << 20, bytes_accessed=1 << 20, transcendentals=0),
        name="moved_attention",
    )(place, queries, queries, *blocks, came, into)


def shift(block, step):
    return lax.ppermute(block, "seq", [(s, s + step) for s in range(8 - step)])


def other_core(block):
    return lax.ppermute(block, "seq", [(s, s ^ 1) for s in range(8)])


def exchange(block, far, two, low_core, cols):
    pair = jnp.concatenate([two[:, cols], jnp.where(low_core, block[:, cols], far[:, cols])], axis=0)
    return block, far, two, other_core(pair)


def body(hidden, queries, keys, frozen_values, labels, partner, down, up):
    place = lax.axis_index("seq").astype(jnp.int32)
    low_core = lax.rem(place, 2) == 0
    place = place.reshape((1,))
    mask = jnp.bitwise_xor(partner[0], lax.axis_index("dp"))
    near, kv_moved, moved_queries, bias_zero, bias_one = adapter(
        place, labels, hidden, frozen_values, keys, down.T, up, queries
    )
    near_two, near_far = shift(near, 2), shift(near, 4)

    def route(m):
        return [(r, r ^ m) for r in range(16)]

    def move(m, kv_moved, moved_queries):
        return lax.ppermute(kv_moved, "dp", route(m)), lax.ppermute(moved_queries, "dp", route(m))

    kv_moved, moved_queries = lax.switch(
        mask - 1, [functools.partial(move, m) for m in range(1, 16)], kv_moved, moved_queries
    )
    kv_moved, moved_queries, near_two, near_far = lax.optimization_barrier(
        (kv_moved, moved_queries, near_two, near_far)
    )
    split = KEPT * 2 * HEAD
    kept_blocks = exchange(near, near_far, near_two, low_core, slice(0, split))
    kept_pair, near_two, near_far = lax.optimization_barrier((kept_blocks[3], near_two, near_far))
    kept_blocks = (near, near_far, near_two, kept_pair)
    zero_blocks = exchange(near, near_far, near_two, low_core, slice(split, None))
    sent = near_attention(
        SMALL_VMEM_LIMIT, 4, 1, 2, KEPT, 0, bias_one, queries, kept_blocks,
        jax.ShapeDtypeStruct((ROWS, KEPT * SPAN), jnp.bfloat16), pl.BlockSpec((ROWS, SPAN), lambda i: (0, i)),
    )

    def send(m, sent, kv_moved, bias, queries, *blocks):
        came = lax.ppermute(sent, "dp", route(m))
        two, far = shift(kv_moved, 2), shift(kv_moved, 4)
        w = lax.ppermute(kv_moved, "seq", [(s, s + 1) for s in range(0, 8, 2)] + [(s, s + 3) for s in range(1, 5, 2)])
        spec = pl.BlockSpec((None, None, ROWS, SPAN), lambda i: (0, 0, 0, i))
        return came, two, far, w, near_attention(VMEM_LIMIT, 2, 0, 1, KV, KEPT, bias, queries, blocks, OUT, spec)

    came, two, far, w, out = lax.switch(
        mask - 1, [functools.partial(send, m) for m in range(1, 16)], sent, kv_moved, bias_zero, queries, *zero_blocks
    )
    moved_blocks = (kv_moved, far, two, other_core(two), w)
    return moved_attention(place, moved_queries, moved_blocks, came, out)


def solution(mesh):
    in_specs = (
        P("dp", None, "seq", None),
        P("dp", None, "seq", None),
        P("dp", None, "seq", None),
        P("dp", None, "seq", None),
        P("dp", None, None),
        P("dp"),
        P(),
        P(),
    )
    out_specs = P("dp", None, "seq", None)
    return jax.shard_map(body, mesh=mesh, in_specs=in_specs, out_specs=out_specs, check_vma=False)
```

```python
import functools

import jax
import jax.numpy as jnp
from jax import lax
from jax.experimental import pallas as pl
from jax.experimental.pallas import tpu as pltpu
from jax.sharding import PartitionSpec as P

HEAD = 128
GROUP = 8
KV = 8
ROWS = 128
SPAN = GROUP * HEAD
PAIR = 2
ADAPTER_SCALE = 2.0
EXP2_SCALE = 1.4426950408889634 / HEAD**0.5
MASKED = -jnp.inf
VMEM_LIMIT = 60 << 20
SMALL_VMEM_LIMIT = 24 << 20

KEPT = KV // 2
MOVED = KV // 2
LABELS_AT = MOVED * 2 * HEAD


def fill_bias(bias_ref, own_at, places, label_at):
    def label_row(at):
        found = jnp.where(at >= 0, label_at(jnp.maximum(at, 0)).astype(jnp.float32), -1.0)
        return jnp.broadcast_to(found, (ROWS, ROWS))

    mine = label_row(own_at)
    query_label = mine.T
    merged = jnp.where(causal(), mine, label_row(own_at - 4))
    for at, tile in enumerate([merged] + [label_row(place) for place in places]):
        bias_ref[at] = jnp.where(tile == query_label, 0.0, MASKED)


def other_places(own_at):
    low_core = lax.rem(own_at, 2) == 0
    return own_at - 2, jnp.where(low_core, own_at - 1, own_at - 3), jnp.where(low_core, own_at - 3, own_at - 1)


def causal():
    rows = lax.broadcasted_iota(jnp.int32, (ROWS, ROWS), 0)
    return lax.broadcasted_iota(jnp.int32, (ROWS, ROWS), 1) <= rows


def adapter_kernel(
    place_ref, labels_ref, hidden_ref, down_ref, frozen_ref, key_ref, up_ref, first_query_ref, second_query_ref,
    near_ref, moved_ref, moved_query_ref, bias_zero_ref, bias_one_ref, low_ref,
):
    step = pl.program_id(0)
    for at, query_ref in enumerate((first_query_ref, second_query_ref)):
        moved_query_ref[:, at * SPAN : (at + 1) * SPAN] = query_ref[...]

    @pl.when(step == 0)
    def _():
        low_ref[...] = jnp.zeros_like(low_ref)
        own_at = place_ref[0]
        for half, bias_ref in enumerate((bias_zero_ref, bias_one_ref)):
            label_at = lambda at: labels_ref[half : half + 1, pl.ds(pl.multiple_of(at * ROWS, ROWS), ROWS)]
            fill_bias(bias_ref, own_at, other_places(own_at), label_at)

    low_ref[...] += lax.dot_general(
        hidden_ref[...].reshape(2 * ROWS, hidden_ref.shape[-1]),
        down_ref[...],
        (((1,), (1,)), ((), ())),
        preferred_element_type=jnp.float32,
    )

    @pl.when(step == pl.num_programs(0) - 1)
    def _():
        low = low_ref[...].astype(jnp.bfloat16)
        delta = jnp.dot(low, up_ref[...], preferred_element_type=jnp.float32)
        for half in range(2):
            own = delta[half * ROWS : (half + 1) * ROWS]
            values = (frozen_ref[half].astype(jnp.float32) + ADAPTER_SCALE * own).astype(jnp.bfloat16)
            for head in range(KV):
                if half == 0:
                    out, at = near_ref, KEPT + head
                else:
                    out, at = (moved_ref if head % 2 else near_ref), head // 2
                cols = slice(head * HEAD, (head + 1) * HEAD)
                out[:, 2 * at * HEAD : (2 * at + 1) * HEAD] = key_ref[half, :, cols]
                out[:, (2 * at + 1) * HEAD : (2 * at + 2) * HEAD] = values[:, cols]
        labels = [labels_ref[1:2, at * ROWS : (at + 1) * ROWS].astype(jnp.float32) for at in range(8)]
        labels = jnp.concatenate(labels + [jnp.zeros((ROWS - 8, HEAD), jnp.float32)], axis=0)
        moved_ref[:, LABELS_AT:] = labels.astype(jnp.bfloat16)


def adapter(place, labels, hidden, frozen_values, keys, down, up, queries):
    width = hidden.shape[-1]
    steps = MOVED // 2
    part = width // steps
    rank = down.shape[0]
    shapes = [
        ((ROWS, (KEPT + KV) * 2 * HEAD), jnp.bfloat16),
        ((ROWS, LABELS_AT + HEAD), jnp.bfloat16),
        ((ROWS, MOVED * SPAN), jnp.bfloat16),
        ((4, ROWS, ROWS), jnp.float32),
        ((4, ROWS, ROWS), jnp.float32),
    ]
    return pl.pallas_call(
        adapter_kernel,
        grid_spec=pltpu.PrefetchScalarGridSpec(
            num_scalar_prefetch=1,
            grid=(steps,),
            in_specs=[
                pl.BlockSpec((None, 2, 8 * ROWS), lambda i, p: (0, 0, 0)),
                pl.BlockSpec((None, 2, ROWS, part), lambda i, p: (0, 0, 0, i)),
                pl.BlockSpec((rank, part), lambda i, p: (0, i)),
                pl.BlockSpec((None, 2, ROWS, KV * HEAD), lambda i, p: (0, 0, 0, 0)),
                pl.BlockSpec((None, 2, ROWS, KV * HEAD), lambda i, p: (0, 0, 0, 0)),
                pl.BlockSpec((rank, KV * HEAD), lambda i, p: (0, 0)),
                pl.BlockSpec((None, None, ROWS, SPAN), lambda i, p: (0, 1, 0, 4 * i + 1)),
                pl.BlockSpec((None, None, ROWS, SPAN), lambda i, p: (0, 1, 0, 4 * i + 3)),
            ],
            out_specs=[
                pl.BlockSpec((ROWS, 2 * SPAN), lambda i, p: (0, i))
                if at == 2
                else pl.BlockSpec(shape, lambda i, p, n=len(shape): (0,) * n)
                for at, (shape, _) in enumerate(shapes)
            ],
            scratch_shapes=[pltpu.VMEM((2 * ROWS, rank), jnp.float32)],
        ),
        out_shape=[jax.ShapeDtypeStruct(*shape) for shape in shapes],
        compiler_params=pltpu.CompilerParams(vmem_limit_bytes=60 << 20),
        cost_estimate=pl.CostEstimate(flops=1 << 20, bytes_accessed=1 << 20, transcendentals=0),
        name="adapter",
    )(place, labels, hidden, down, frozen_values, keys, up, queries, queries)


def near_attention_kernel(unroll, bias_ref, query_ref, own_ref, far_ref, two_ref, pair_ref, out_ref, key_ref, value_ref):
    attend(unroll, bias_ref, query_ref, (own_ref, far_ref, two_ref, pair_ref), out_ref, 0, key_ref, value_ref)


def moved_attention_kernel(
    unroll, place_ref, label_ref, query_ref, own_ref, far_ref, two_ref, x_ref, w_ref, came_ref, _,
    out_ref, bias_ref, key_ref, value_ref,
):
    @pl.when(pl.program_id(0) == 0)
    def _():
        own_at = place_ref[0]
        rows = label_ref[...].astype(jnp.float32)
        chosen = lax.broadcasted_iota(jnp.int32, rows.shape, 0)

        def label_at(at):
            return jnp.sum(jnp.where(chosen == at, rows, 0.0), axis=0, keepdims=True)

        fill_bias(bias_ref, own_at, other_places(own_at), label_at)

    out_ref[:, :SPAN] = came_ref[...]
    attend(unroll, bias_ref, query_ref, (own_ref, far_ref, two_ref, x_ref, w_ref), out_ref, GROUP, key_ref, value_ref)


def attend(unroll, bias_ref, query_ref, blocks, out_ref, out_head, key_ref, value_ref):
    is_causal = causal()

    @pl.when(pl.program_id(0) == 0)
    def _():
        value_ref[:, HEAD:] = jnp.ones((5 * ROWS, HEAD), jnp.bfloat16)

    at = 0
    for block in blocks:
        span = slice(at, at + block.shape[0])
        key_ref[span, :] = block[:, :HEAD]
        value_ref[span, :HEAD] = block[:, HEAD:]
        at += block.shape[0]

    def some_heads(step, carry):
        spans = [pl.ds(pl.multiple_of((step * PAIR + i) * HEAD, HEAD), HEAD) for i in range(PAIR)]
        queries = jnp.concatenate([query_ref[:, span] for span in spans], axis=0)
        scores = lax.dot_general(
            queries, key_ref[...], (((1,), (1,)), ((), ())), preferred_element_type=jnp.float32
        )
        weights = []
        for i in range(PAIR):
            mine = scores[i * ROWS : (i + 1) * ROWS]
            tiles = [jnp.where(is_causal, mine[:, :ROWS], mine[:, ROWS : 2 * ROWS]) + bias_ref[0]]
            tiles += [mine[:, (t + 1) * ROWS : (t + 2) * ROWS] + bias_ref[t] for t in range(1, 4)]
            peak = jnp.maximum(jnp.maximum(tiles[0], tiles[1]), jnp.maximum(tiles[2], tiles[3]))
            peak = jnp.max(peak, axis=1, keepdims=True)
            raised = [jnp.exp2((tile - peak) * EXP2_SCALE) for tile in tiles]
            near = jnp.where(is_causal, raised[0], 0.0).astype(jnp.bfloat16)
            far = jnp.where(is_causal, 0.0, raised[0]).astype(jnp.bfloat16)
            weights.append(
                jnp.concatenate([near, far] + [r.astype(jnp.bfloat16) for r in raised[1:]], axis=1)
            )
        blended = jnp.dot(
            jnp.concatenate(weights, axis=0), value_ref[...], preferred_element_type=jnp.float32
        )
        result = (blended[:, :HEAD] / blended[:, HEAD:]).astype(jnp.bfloat16)
        for i in range(PAIR):
            span = pl.ds(pl.multiple_of((out_head + step * PAIR + i) * HEAD, HEAD), HEAD)
            out_ref[:, span] = result[i * ROWS : (i + 1) * ROWS]
        return carry

    steps = GROUP // PAIR
    if unroll == steps:
        for step in range(steps):
            some_heads(step, 0)
    else:
        lax.fori_loop(0, steps, some_heads, 0, unroll=unroll)


SCRATCH = [pltpu.VMEM((5 * ROWS, HEAD), jnp.bfloat16), pltpu.VMEM((5 * ROWS, 2 * HEAD), jnp.bfloat16)]
OUT = jax.ShapeDtypeStruct((1, 2, ROWS, KV * SPAN), jnp.bfloat16)


def block_specs(first):
    whole = pl.BlockSpec((ROWS, 2 * HEAD), lambda i, *p: (0, first + i))
    return [whole, whole, whole, pl.BlockSpec((2 * ROWS, 2 * HEAD), lambda i, *p: (0, i))]


def near_attention(vmem_limit, unroll, half, stride, count, first, bias, queries, blocks, out_shape, out_spec):
    return pl.pallas_call(
        functools.partial(near_attention_kernel, unroll),
        grid=(count,),
        in_specs=[
            pl.BlockSpec((4, ROWS, ROWS), lambda i: (0, 0, 0)),
            pl.BlockSpec((None, None, ROWS, SPAN), lambda i: (0, half, 0, stride * i)),
        ]
        + block_specs(first),
        out_specs=out_spec,
        scratch_shapes=SCRATCH,
        out_shape=out_shape,
        compiler_params=pltpu.CompilerParams(vmem_limit_bytes=vmem_limit),
        cost_estimate=pl.CostEstimate(flops=1 << 20, bytes_accessed=1 << 20, transcendentals=0),
        name="near_attention",
    )(bias, queries, *blocks)


def moved_attention(place, queries, blocks, came, into):
    return pl.pallas_call(
        functools.partial(moved_attention_kernel, 4),
        grid_spec=pltpu.PrefetchScalarGridSpec(
            num_scalar_prefetch=1,
            grid=(MOVED,),
            in_specs=[
                pl.BlockSpec((16, HEAD), lambda i, p: (0, LABELS_AT // HEAD)),
                pl.BlockSpec((ROWS, SPAN), lambda i, p: (0, i)),
            ]
            + [pl.BlockSpec((ROWS, 2 * HEAD), lambda i, p: (0, i))] * 5
            + [pl.BlockSpec((ROWS, SPAN), lambda i, p: (0, i)), pl.BlockSpec(memory_space=pl.ANY)],
            out_specs=pl.BlockSpec((None, None, ROWS, 2 * SPAN), lambda i, p: (0, 1, 0, i)),
            scratch_shapes=[pltpu.VMEM((4, ROWS, ROWS), jnp.float32)] + SCRATCH,
        ),
        out_shape=OUT,
        input_output_aliases={9: 0},
        compiler_params=pltpu.CompilerParams(vmem_limit_bytes=SMALL_VMEM_LIMIT),
        cost_estimate=pl.CostEstimate(flops=1 << 20, bytes_accessed=1 << 20, transcendentals=0),
        name="moved_attention",
    )(place, blocks[0], queries, *blocks, came, into)


def shift(block, step, odd_step=None, wrap=False):
    route = [(s, s + (step if odd_step is None or s % 2 == 0 else odd_step)) for s in range(8)]
    return lax.ppermute(block, "seq", [(s, t % 8) for s, t in route if wrap or t < 8])


def other_core(block):
    return lax.ppermute(block, "seq", [(s, s ^ 1) for s in range(8)])


def exchange(block, far, two, low_core, cols):
    pair = jnp.concatenate([two[:, cols], jnp.where(low_core, block[:, cols], far[:, cols])], axis=0)
    return block, far, two, other_core(pair)


def body(hidden, queries, keys, frozen_values, labels, partner, down, up):
    place = lax.axis_index("seq").astype(jnp.int32)
    low_core = lax.rem(place, 2) == 0
    place = place.reshape((1,))
    mask = jnp.bitwise_xor(partner[0], lax.axis_index("dp"))
    near, kv_moved, moved_queries, bias_zero, bias_one = adapter(
        place, labels, hidden, frozen_values, keys, down.T, up, queries
    )
    near_two, near_far = shift(near, 2, wrap=True), shift(near, 4, wrap=True)

    def route(m):
        return [(r, r ^ m) for r in range(16)]

    def move(m, kv_moved, moved_queries):
        return lax.ppermute(kv_moved, "dp", route(m)), lax.ppermute(moved_queries, "dp", route(m))

    kv_moved, moved_queries = lax.switch(
        mask - 1, [functools.partial(move, m) for m in range(1, 16)], kv_moved, moved_queries
    )
    kv_moved, moved_queries, near_two, near_far = lax.optimization_barrier(
        (kv_moved, moved_queries, near_two, near_far)
    )
    w = shift(kv_moved, 1, 3, wrap=True)
    split = KEPT * 2 * HEAD
    kept_blocks = exchange(near, near_far, near_two, low_core, slice(0, split))
    kept_pair, near_two, near_far = lax.optimization_barrier((kept_blocks[3], near_two, near_far))
    kept_blocks = (near, near_far, near_two, kept_pair)
    zero_blocks = exchange(near, near_far, near_two, low_core, slice(split, None))
    sent = near_attention(
        SMALL_VMEM_LIMIT, 4, 1, 2, KEPT, 0, bias_one, queries, kept_blocks,
        jax.ShapeDtypeStruct((ROWS, KEPT * SPAN), jnp.bfloat16), pl.BlockSpec((ROWS, SPAN), lambda i: (0, i)),
    )

    def send(m, sent, kv_moved, bias, queries, *blocks):
        came = lax.ppermute(sent, "dp", route(m))
        two, far, x = shift(kv_moved, 2), shift(kv_moved, 4), shift(kv_moved, 3, 1)
        spec = pl.BlockSpec((None, None, ROWS, SPAN), lambda i: (0, 0, 0, i))
        return came, two, far, x, near_attention(VMEM_LIMIT, 2, 0, 1, KV, KEPT, bias, queries, blocks, OUT, spec)

    came, two, far, x, out = lax.switch(
        mask - 1, [functools.partial(send, m) for m in range(1, 16)], sent, kv_moved, bias_zero, queries, *zero_blocks
    )
    moved_blocks = (kv_moved, far, two, x, w)
    return moved_attention(place, moved_queries, moved_blocks, came, out)


def solution(mesh):
    in_specs = (
        P("dp", None, "seq", None),
        P("dp", None, "seq", None),
        P("dp", None, "seq", None),
        P("dp", None, "seq", None),
        P("dp", None, None),
        P("dp"),
        P(),
        P(),
    )
    out_specs = P("dp", None, "seq", None)
    return jax.shard_map(body, mesh=mesh, in_specs=in_specs, out_specs=out_specs, check_vma=False)
```

```python
import functools

import jax
import jax.numpy as jnp
from jax import lax
from jax.experimental import pallas as pl
from jax.experimental.pallas import tpu as pltpu
from jax.sharding import PartitionSpec as P

HEAD = 128
GROUP = 8
KV = 8
ROWS = 128
SPAN = GROUP * HEAD
PAIR = 2
ADAPTER_SCALE = 2.0
EXP2_SCALE = 1.4426950408889634 / HEAD**0.5
MASKED = -jnp.inf
VMEM_LIMIT = 60 << 20
SMALL_VMEM_LIMIT = 24 << 20

KEPT = KV // 2
MOVED = KV // 2
LABELS_AT = MOVED * 2 * ROWS
LABEL_ROWS = 16


def fill_bias(bias_ref, own_at, places, label_at, by_key):
    def label_row(at):
        found = jnp.where(at >= 0, label_at(jnp.maximum(at, 0)).astype(jnp.float32), -1.0)
        return jnp.broadcast_to(found, (ROWS, ROWS))

    mine = label_row(own_at)
    query_label = mine.T
    merged = jnp.where(causal(), mine, label_row(own_at - 4))
    for at, tile in enumerate([merged] + [label_row(place) for place in places]):
        bias = jnp.where(tile == query_label, 0.0, MASKED)
        bias_ref[at] = bias.T if by_key else bias


def other_places(own_at):
    low_core = lax.rem(own_at, 2) == 0
    return own_at - 2, jnp.where(low_core, own_at - 1, own_at - 3), jnp.where(low_core, own_at - 3, own_at - 1)


def causal():
    rows = lax.broadcasted_iota(jnp.int32, (ROWS, ROWS), 0)
    return lax.broadcasted_iota(jnp.int32, (ROWS, ROWS), 1) <= rows


def adapter_kernel(
    place_ref, labels_ref, hidden_ref, down_ref, frozen_ref, key_ref, up_ref, first_query_ref, second_query_ref,
    near_ref, moved_ref, moved_query_ref, bias_zero_ref, bias_one_ref, low_ref,
):
    step = pl.program_id(0)
    for at, query_ref in enumerate((first_query_ref, second_query_ref)):
        moved_query_ref[:, at * SPAN : (at + 1) * SPAN] = query_ref[...]

    @pl.when(step == 0)
    def _():
        low_ref[...] = jnp.zeros_like(low_ref)
        own_at = place_ref[0]
        for half, bias_ref in enumerate((bias_zero_ref, bias_one_ref)):
            label_at = lambda at: labels_ref[half : half + 1, pl.ds(pl.multiple_of(at * ROWS, ROWS), ROWS)]
            fill_bias(bias_ref, own_at, other_places(own_at), label_at, half == 1)

    low_ref[...] += lax.dot_general(
        hidden_ref[...].reshape(2 * ROWS, hidden_ref.shape[-1]),
        down_ref[...],
        (((1,), (1,)), ((), ())),
        preferred_element_type=jnp.float32,
    )

    @pl.when(step == pl.num_programs(0) - 1)
    def _():
        low = low_ref[...].astype(jnp.bfloat16)
        delta = jnp.dot(low, up_ref[...], preferred_element_type=jnp.float32)
        for half in range(2):
            own = delta[half * ROWS : (half + 1) * ROWS]
            values = (frozen_ref[half].astype(jnp.float32) + ADAPTER_SCALE * own).astype(jnp.bfloat16)
            for head in range(KV):
                cols = slice(head * HEAD, (head + 1) * HEAD)
                key = key_ref[half, :, cols]
                value = values[:, cols]
                if half == 1 and head % 2 == 1:
                    at = (head - 1) * ROWS
                    moved_ref[at : at + ROWS, :] = key
                    moved_ref[at + ROWS : at + 2 * ROWS, :] = value
                else:
                    at = (head if half == 1 else 2 * (KEPT + head)) * HEAD
                    near_ref[:, at : at + HEAD] = key
                    near_ref[:, at + HEAD : at + 2 * HEAD] = value
        labels = [labels_ref[1:2, at * ROWS : (at + 1) * ROWS].astype(jnp.float32) for at in range(8)]
        labels = jnp.concatenate(labels + [jnp.zeros((LABEL_ROWS - 8, HEAD), jnp.float32)], axis=0)
        moved_ref[LABELS_AT:, :] = labels.astype(jnp.bfloat16)


def adapter(place, labels, hidden, frozen_values, keys, down, up, queries):
    width = hidden.shape[-1]
    steps = MOVED // 2
    part = width // steps
    rank = down.shape[0]
    shapes = [
        ((ROWS, (KEPT + KV) * 2 * HEAD), jnp.bfloat16),
        ((LABELS_AT + LABEL_ROWS, HEAD), jnp.bfloat16),
        ((ROWS, MOVED * SPAN), jnp.bfloat16),
        ((4, ROWS, ROWS), jnp.float32),
        ((4, ROWS, ROWS), jnp.float32),
    ]
    return pl.pallas_call(
        adapter_kernel,
        grid_spec=pltpu.PrefetchScalarGridSpec(
            num_scalar_prefetch=1,
            grid=(steps,),
            in_specs=[
                pl.BlockSpec((None, 2, 8 * ROWS), lambda i, p: (0, 0, 0)),
                pl.BlockSpec((None, 2, ROWS, part), lambda i, p: (0, 0, 0, i)),
                pl.BlockSpec((rank, part), lambda i, p: (0, i)),
                pl.BlockSpec((None, 2, ROWS, KV * HEAD), lambda i, p: (0, 0, 0, 0)),
                pl.BlockSpec((None, 2, ROWS, KV * HEAD), lambda i, p: (0, 0, 0, 0)),
                pl.BlockSpec((rank, KV * HEAD), lambda i, p: (0, 0)),
                pl.BlockSpec((None, None, ROWS, SPAN), lambda i, p: (0, 1, 0, 4 * i + 1)),
                pl.BlockSpec((None, None, ROWS, SPAN), lambda i, p: (0, 1, 0, 4 * i + 3)),
            ],
            out_specs=[
                pl.BlockSpec((ROWS, 2 * SPAN), lambda i, p: (0, i))
                if at == 2
                else pl.BlockSpec(shape, lambda i, p, n=len(shape): (0,) * n)
                for at, (shape, _) in enumerate(shapes)
            ],
            scratch_shapes=[pltpu.VMEM((2 * ROWS, rank), jnp.float32)],
        ),
        out_shape=[jax.ShapeDtypeStruct(*shape) for shape in shapes],
        compiler_params=pltpu.CompilerParams(vmem_limit_bytes=60 << 20),
        cost_estimate=pl.CostEstimate(flops=1 << 20, bytes_accessed=1 << 20, transcendentals=0),
        name="adapter",
    )(place, labels, hidden, down, frozen_values, keys, up, queries, queries)


def near_attention_kernel(by_key, bias_ref, query_ref, own_ref, far_ref, two_ref, pair_ref, out_ref, key_ref, value_ref):
    blocks = [(block, (at, 0), (at, HEAD)) for block, at in ((own_ref, 0), (far_ref, 0), (two_ref, 0), (pair_ref, 0), (pair_ref, ROWS))]
    attend = attend_by_key if by_key else attend_by_query
    attend(bias_ref, query_ref, blocks, out_ref, 0, key_ref, value_ref)


def moved_attention_kernel(
    place_ref, label_ref, query_ref, own_ref, far_ref, two_ref, x_ref, w_ref, came_ref, _,
    out_ref, bias_ref, key_ref, value_ref,
):
    @pl.when(pl.program_id(0) == 0)
    def _():
        own_at = place_ref[0]
        rows = label_ref[...].astype(jnp.float32)
        chosen = lax.broadcasted_iota(jnp.int32, rows.shape, 0)

        def label_at(at):
            return jnp.sum(jnp.where(chosen == at, rows, 0.0), axis=0, keepdims=True)

        fill_bias(bias_ref, own_at, other_places(own_at), label_at, True)

    out_ref[:, :SPAN] = came_ref[...]
    blocks = [(block, (0, 0), (ROWS, 0)) for block in (own_ref, far_ref, two_ref, x_ref, w_ref)]
    attend_by_key(bias_ref, query_ref, blocks, out_ref, GROUP, key_ref, value_ref)


def tile_of(block, corner):
    return block[corner[0] : corner[0] + ROWS, corner[1] : corner[1] + HEAD]


def attend_by_key(bias_ref, query_ref, blocks, out_ref, out_head, key_ref, value_ref):
    is_causal = causal().T

    @pl.when(pl.program_id(0) == 0)
    def _():
        value_ref[HEAD:, :] = jnp.ones((ONES, 5 * ROWS), jnp.bfloat16)

    for at, (block, key_at, value_at) in enumerate(blocks):
        span = slice(at * ROWS, (at + 1) * ROWS)
        key_ref[span, :] = tile_of(block, key_at)
        value_ref[:HEAD, span] = tile_of(block, value_at).T
    queries = jnp.concatenate([query_ref[:, i * HEAD : (i + 1) * HEAD] for i in range(GROUP)], axis=0)
    scores = lax.dot_general(key_ref[...], queries, (((1,), (1,)), ((), ())), preferred_element_type=jnp.float32)
    weights = []
    for i in range(GROUP):
        mine = scores[:, i * ROWS : (i + 1) * ROWS]
        tiles = [jnp.where(is_causal, mine[:ROWS], mine[ROWS : 2 * ROWS]) + bias_ref[0]]
        tiles += [mine[(t + 1) * ROWS : (t + 2) * ROWS] + bias_ref[t] for t in range(1, 4)]
        peak = jnp.maximum(jnp.maximum(tiles[0], tiles[1]), jnp.maximum(tiles[2], tiles[3]))
        peak = jnp.max(peak, axis=0, keepdims=True)
        raised = [jnp.exp2((tile - peak) * EXP2_SCALE) for tile in tiles]
        near = jnp.where(is_causal, raised[0], 0.0).astype(jnp.bfloat16)
        far = jnp.where(is_causal, 0.0, raised[0]).astype(jnp.bfloat16)
        weights.append(jnp.concatenate([near, far] + [r.astype(jnp.bfloat16) for r in raised[1:]], axis=0))
    blended = jnp.dot(value_ref[...], jnp.concatenate(weights, axis=1), preferred_element_type=jnp.float32)
    result = blended[:HEAD] / blended[HEAD : HEAD + 1]
    for i in range(GROUP):
        at = (out_head + i) * HEAD
        out_ref[:, at : at + HEAD] = result[:, i * ROWS : (i + 1) * ROWS].T.astype(jnp.bfloat16)


def attend_by_query(bias_ref, query_ref, blocks, out_ref, out_head, key_ref, value_ref):
    is_causal = causal()

    @pl.when(pl.program_id(0) == 0)
    def _():
        value_ref[:, HEAD:] = jnp.ones((5 * ROWS, HEAD), jnp.bfloat16)

    for at, (block, key_at, value_at) in enumerate(blocks):
        span = slice(at * ROWS, (at + 1) * ROWS)
        key_ref[span, :] = tile_of(block, key_at)
        value_ref[span, :HEAD] = tile_of(block, value_at)

    def some_heads(step, carry):
        spans = [pl.ds(pl.multiple_of((step * PAIR + i) * HEAD, HEAD), HEAD) for i in range(PAIR)]
        queries = jnp.concatenate([query_ref[:, span] for span in spans], axis=0)
        scores = lax.dot_general(
            queries, key_ref[...], (((1,), (1,)), ((), ())), preferred_element_type=jnp.float32
        )
        weights = []
        for i in range(PAIR):
            mine = scores[i * ROWS : (i + 1) * ROWS]
            tiles = [jnp.where(is_causal, mine[:, :ROWS], mine[:, ROWS : 2 * ROWS]) + bias_ref[0]]
            tiles += [mine[:, (t + 1) * ROWS : (t + 2) * ROWS] + bias_ref[t] for t in range(1, 4)]
            peak = jnp.maximum(jnp.maximum(tiles[0], tiles[1]), jnp.maximum(tiles[2], tiles[3]))
            peak = jnp.max(peak, axis=1, keepdims=True)
            raised = [jnp.exp2((tile - peak) * EXP2_SCALE) for tile in tiles]
            near = jnp.where(is_causal, raised[0], 0.0).astype(jnp.bfloat16)
            far = jnp.where(is_causal, 0.0, raised[0]).astype(jnp.bfloat16)
            weights.append(
                jnp.concatenate([near, far] + [r.astype(jnp.bfloat16) for r in raised[1:]], axis=1)
            )
        blended = jnp.dot(
            jnp.concatenate(weights, axis=0), value_ref[...], preferred_element_type=jnp.float32
        )
        result = (blended[:, :HEAD] / blended[:, HEAD:]).astype(jnp.bfloat16)
        for i in range(PAIR):
            span = pl.ds(pl.multiple_of((out_head + step * PAIR + i) * HEAD, HEAD), HEAD)
            out_ref[:, span] = result[i * ROWS : (i + 1) * ROWS]
        return carry

    lax.fori_loop(0, GROUP // PAIR, some_heads, 0, unroll=2)


ONES = 16
BY_QUERY_SCRATCH = [pltpu.VMEM((5 * ROWS, HEAD), jnp.bfloat16), pltpu.VMEM((5 * ROWS, 2 * HEAD), jnp.bfloat16)]
BY_KEY_SCRATCH = [pltpu.VMEM((5 * ROWS, HEAD), jnp.bfloat16), pltpu.VMEM((HEAD + ONES, 5 * ROWS), jnp.bfloat16)]
OUT = jax.ShapeDtypeStruct((1, 2, ROWS, KV * SPAN), jnp.bfloat16)


def block_specs(first):
    whole = pl.BlockSpec((ROWS, 2 * HEAD), lambda i, *p: (0, first + i))
    return [whole, whole, whole, pl.BlockSpec((2 * ROWS, 2 * HEAD), lambda i, *p: (0, i))]


def near_attention(vmem_limit, by_key, half, stride, count, first, bias, queries, blocks, out_shape, out_spec):
    return pl.pallas_call(
        functools.partial(near_attention_kernel, by_key),
        grid=(count,),
        in_specs=[
            pl.BlockSpec((4, ROWS, ROWS), lambda i: (0, 0, 0)),
            pl.BlockSpec((None, None, ROWS, SPAN), lambda i: (0, half, 0, stride * i)),
        ]
        + block_specs(first),
        out_specs=out_spec,
        scratch_shapes=BY_KEY_SCRATCH if by_key else BY_QUERY_SCRATCH,
        out_shape=out_shape,
        compiler_params=pltpu.CompilerParams(vmem_limit_bytes=vmem_limit),
        cost_estimate=pl.CostEstimate(flops=1 << 20, bytes_accessed=1 << 20, transcendentals=0),
        name="near_attention",
    )(bias, queries, *blocks)


def moved_attention(place, queries, blocks, came, into):
    return pl.pallas_call(
        moved_attention_kernel,
        grid_spec=pltpu.PrefetchScalarGridSpec(
            num_scalar_prefetch=1,
            grid=(MOVED,),
            in_specs=[
                pl.BlockSpec((LABEL_ROWS, HEAD), lambda i, p: (LABELS_AT // LABEL_ROWS, 0)),
                pl.BlockSpec((ROWS, SPAN), lambda i, p: (0, i)),
            ]
            + [pl.BlockSpec((2 * ROWS, HEAD), lambda i, p: (i, 0))] * 5
            + [pl.BlockSpec((ROWS, SPAN), lambda i, p: (0, i)), pl.BlockSpec(memory_space=pl.ANY)],
            out_specs=pl.BlockSpec((None, None, ROWS, 2 * SPAN), lambda i, p: (0, 1, 0, i)),
            scratch_shapes=[pltpu.VMEM((4, ROWS, ROWS), jnp.float32)] + BY_KEY_SCRATCH,
        ),
        out_shape=OUT,
        input_output_aliases={9: 0},
        compiler_params=pltpu.CompilerParams(vmem_limit_bytes=SMALL_VMEM_LIMIT),
        cost_estimate=pl.CostEstimate(flops=1 << 20, bytes_accessed=1 << 20, transcendentals=0),
        name="moved_attention",
    )(place, blocks[0], queries, *blocks, came, into)


def shift(block, step, odd_step=None, wrap=False):
    route = [(s, s + (step if odd_step is None or s % 2 == 0 else odd_step)) for s in range(8)]
    return lax.ppermute(block, "seq", [(s, t % 8) for s, t in route if wrap or t < 8])


def other_core(block):
    return lax.ppermute(block, "seq", [(s, s ^ 1) for s in range(8)])


def exchange(block, far, two, low_core, cols):
    pair = jnp.concatenate([two[:, cols], jnp.where(low_core, block[:, cols], far[:, cols])], axis=0)
    return block, far, two, other_core(pair)


def body(hidden, queries, keys, frozen_values, labels, partner, down, up):
    place = lax.axis_index("seq").astype(jnp.int32)
    low_core = lax.rem(place, 2) == 0
    place = place.reshape((1,))
    mask = jnp.bitwise_xor(partner[0], lax.axis_index("dp"))
    near, kv_moved, moved_queries, bias_zero, bias_one = adapter(
        place, labels, hidden, frozen_values, keys, down.T, up, queries
    )
    near_two, near_far = shift(near, 2, wrap=True), shift(near, 4, wrap=True)

    def route(m):
        return [(r, r ^ m) for r in range(16)]

    def move(m, kv_moved, moved_queries):
        return lax.ppermute(kv_moved, "dp", route(m)), lax.ppermute(moved_queries, "dp", route(m))

    kv_moved, moved_queries = lax.switch(
        mask - 1, [functools.partial(move, m) for m in range(1, 16)], kv_moved, moved_queries
    )
    kv_moved, moved_queries, near_two, near_far = lax.optimization_barrier(
        (kv_moved, moved_queries, near_two, near_far)
    )
    w = shift(kv_moved, 1, 3, wrap=True)
    split = KEPT * 2 * HEAD
    kept_blocks = exchange(near, near_far, near_two, low_core, slice(0, split))
    kept_pair, near_two, near_far = lax.optimization_barrier((kept_blocks[3], near_two, near_far))
    kept_blocks = (near, near_far, near_two, kept_pair)
    zero_blocks = exchange(near, near_far, near_two, low_core, slice(split, None))
    sent = near_attention(
        SMALL_VMEM_LIMIT, True, 1, 2, KEPT, 0, bias_one, queries, kept_blocks,
        jax.ShapeDtypeStruct((ROWS, KEPT * SPAN), jnp.bfloat16), pl.BlockSpec((ROWS, SPAN), lambda i: (0, i)),
    )

    def send(m, sent, kv_moved, bias, queries, *blocks):
        came = lax.ppermute(sent, "dp", route(m))
        two, far, x = shift(kv_moved, 2), shift(kv_moved, 4), shift(kv_moved, 3, 1)
        spec = pl.BlockSpec((None, None, ROWS, SPAN), lambda i: (0, 0, 0, i))
        return came, two, far, x, near_attention(VMEM_LIMIT, False, 0, 1, KV, KEPT, bias, queries, blocks, OUT, spec)

    came, two, far, x, out = lax.switch(
        mask - 1, [functools.partial(send, m) for m in range(1, 16)], sent, kv_moved, bias_zero, queries, *zero_blocks
    )
    moved_blocks = (kv_moved, far, two, x, w)
    return moved_attention(place, moved_queries, moved_blocks, came, out)


def solution(mesh):
    in_specs = (
        P("dp", None, "seq", None),
        P("dp", None, "seq", None),
        P("dp", None, "seq", None),
        P("dp", None, "seq", None),
        P("dp", None, None),
        P("dp"),
        P(),
        P(),
    )
    out_specs = P("dp", None, "seq", None)
    return jax.shard_map(body, mesh=mesh, in_specs=in_specs, out_specs=out_specs, check_vma=False)
```

```python
import functools

import jax
import jax.numpy as jnp
from jax import lax
from jax.experimental import pallas as pl
from jax.experimental.pallas import tpu as pltpu
from jax.sharding import PartitionSpec as P

HEAD = 128
GROUP = 8
KV = 8
ROWS = 128
SPAN = GROUP * HEAD
PAIR = 2
ADAPTER_SCALE = 2.0
EXP2_SCALE = 1.4426950408889634 / HEAD**0.5
MASKED = -jnp.inf
VMEM_LIMIT = 60 << 20
SMALL_VMEM_LIMIT = 24 << 20

KEPT = KV // 2
MOVED = KV // 2
LABELS_AT = MOVED * 2 * ROWS
LABEL_ROWS = 16


def fill_bias(bias_ref, own_at, places, label_at, by_key):
    def label_row(at):
        found = jnp.where(at >= 0, label_at(jnp.maximum(at, 0)).astype(jnp.float32), -1.0)
        return jnp.broadcast_to(found, (ROWS, ROWS))

    mine = label_row(own_at)
    query_label = mine.T
    merged = jnp.where(causal(), mine, label_row(own_at - 4))
    for at, tile in enumerate([merged] + [label_row(place) for place in places]):
        bias = jnp.where(tile == query_label, 0.0, MASKED)
        bias_ref[at] = bias.T if by_key else bias


def other_places(own_at):
    low_core = lax.rem(own_at, 2) == 0
    return own_at - 2, jnp.where(low_core, own_at - 1, own_at - 3), jnp.where(low_core, own_at - 3, own_at - 1)


def causal():
    rows = lax.broadcasted_iota(jnp.int32, (ROWS, ROWS), 0)
    return lax.broadcasted_iota(jnp.int32, (ROWS, ROWS), 1) <= rows


def adapter_kernel(
    place_ref, labels_ref, hidden_ref, down_ref, frozen_ref, key_ref, up_ref, first_query_ref, second_query_ref,
    near_ref, moved_ref, moved_query_ref, bias_zero_ref, bias_one_ref, low_ref,
):
    step = pl.program_id(0)
    for at, query_ref in enumerate((first_query_ref, second_query_ref)):
        moved_query_ref[:, at * SPAN : (at + 1) * SPAN] = query_ref[...]

    @pl.when(step == 0)
    def _():
        low_ref[...] = jnp.zeros_like(low_ref)
        own_at = place_ref[0]
        for half, bias_ref in enumerate((bias_zero_ref, bias_one_ref)):
            label_at = lambda at: labels_ref[half : half + 1, pl.ds(pl.multiple_of(at * ROWS, ROWS), ROWS)]
            fill_bias(bias_ref, own_at, other_places(own_at), label_at, half == 1)

    low_ref[...] += lax.dot_general(
        hidden_ref[...].reshape(2 * ROWS, hidden_ref.shape[-1]),
        down_ref[...],
        (((1,), (1,)), ((), ())),
        preferred_element_type=jnp.float32,
    )

    @pl.when(step == pl.num_programs(0) - 1)
    def _():
        low = low_ref[...].astype(jnp.bfloat16)
        delta = jnp.dot(low, up_ref[...], preferred_element_type=jnp.float32)
        for half in range(2):
            own = delta[half * ROWS : (half + 1) * ROWS]
            values = (frozen_ref[half].astype(jnp.float32) + ADAPTER_SCALE * own).astype(jnp.bfloat16)
            for head in range(KV):
                cols = slice(head * HEAD, (head + 1) * HEAD)
                key = key_ref[half, :, cols]
                value = values[:, cols]
                if half == 1 and head % 2 == 1:
                    at = (head - 1) * ROWS
                    moved_ref[at : at + ROWS, :] = key
                    moved_ref[at + ROWS : at + 2 * ROWS, :] = value
                else:
                    at = (head if half == 1 else 2 * (KEPT + head)) * HEAD
                    near_ref[:, at : at + HEAD] = key
                    near_ref[:, at + HEAD : at + 2 * HEAD] = value
        labels = [labels_ref[1:2, at * ROWS : (at + 1) * ROWS].astype(jnp.float32) for at in range(8)]
        labels = jnp.concatenate(labels + [jnp.zeros((LABEL_ROWS - 8, HEAD), jnp.float32)], axis=0)
        moved_ref[LABELS_AT:, :] = labels.astype(jnp.bfloat16)


def adapter(place, labels, hidden, frozen_values, keys, down, up, queries):
    width = hidden.shape[-1]
    steps = MOVED // 2
    part = width // steps
    rank = down.shape[0]
    shapes = [
        ((ROWS, (KEPT + KV) * 2 * HEAD), jnp.bfloat16),
        ((LABELS_AT + LABEL_ROWS, HEAD), jnp.bfloat16),
        ((ROWS, MOVED * SPAN), jnp.bfloat16),
        ((4, ROWS, ROWS), jnp.float32),
        ((4, ROWS, ROWS), jnp.float32),
    ]
    return pl.pallas_call(
        adapter_kernel,
        grid_spec=pltpu.PrefetchScalarGridSpec(
            num_scalar_prefetch=1,
            grid=(steps,),
            in_specs=[
                pl.BlockSpec((None, 2, 8 * ROWS), lambda i, p: (0, 0, 0)),
                pl.BlockSpec((None, 2, ROWS, part), lambda i, p: (0, 0, 0, i)),
                pl.BlockSpec((rank, part), lambda i, p: (0, i)),
                pl.BlockSpec((None, 2, ROWS, KV * HEAD), lambda i, p: (0, 0, 0, 0)),
                pl.BlockSpec((None, 2, ROWS, KV * HEAD), lambda i, p: (0, 0, 0, 0)),
                pl.BlockSpec((rank, KV * HEAD), lambda i, p: (0, 0)),
                pl.BlockSpec((None, None, ROWS, SPAN), lambda i, p: (0, 1, 0, 4 * i + 1)),
                pl.BlockSpec((None, None, ROWS, SPAN), lambda i, p: (0, 1, 0, 4 * i + 3)),
            ],
            out_specs=[
                pl.BlockSpec((ROWS, 2 * SPAN), lambda i, p: (0, i))
                if at == 2
                else pl.BlockSpec(shape, lambda i, p, n=len(shape): (0,) * n)
                for at, (shape, _) in enumerate(shapes)
            ],
            scratch_shapes=[pltpu.VMEM((2 * ROWS, rank), jnp.float32)],
        ),
        out_shape=[jax.ShapeDtypeStruct(*shape) for shape in shapes],
        compiler_params=pltpu.CompilerParams(vmem_limit_bytes=60 << 20),
        cost_estimate=pl.CostEstimate(flops=1 << 20, bytes_accessed=1 << 20, transcendentals=0),
        name="adapter",
    )(place, labels, hidden, down, frozen_values, keys, up, queries, queries)


def near_attention_kernel(by_key, bias_ref, query_ref, own_ref, far_ref, two_ref, pair_ref, out_ref, key_ref, value_ref):
    blocks = [(block, (at, 0), (at, HEAD)) for block, at in ((own_ref, 0), (far_ref, 0), (two_ref, 0), (pair_ref, 0), (pair_ref, ROWS))]
    attend = attend_by_key if by_key else attend_by_query
    attend(bias_ref, query_ref, blocks, out_ref, 0, key_ref, value_ref)


def moved_attention_kernel(
    place_ref, label_ref, query_ref, own_ref, far_ref, two_ref, x_ref, w_ref, came_ref, _,
    out_ref, bias_ref, key_ref, value_ref,
):
    @pl.when(pl.program_id(0) == 0)
    def _():
        own_at = place_ref[0]
        rows = label_ref[...].astype(jnp.float32)
        chosen = lax.broadcasted_iota(jnp.int32, rows.shape, 0)

        def label_at(at):
            return jnp.sum(jnp.where(chosen == at, rows, 0.0), axis=0, keepdims=True)

        fill_bias(bias_ref, own_at, other_places(own_at), label_at, True)

    out_ref[:, :SPAN] = came_ref[...]
    blocks = [(block, (0, 0), (ROWS, 0)) for block in (own_ref, far_ref, two_ref, x_ref, w_ref)]
    attend_by_key(bias_ref, query_ref, blocks, out_ref, GROUP, key_ref, value_ref)


def tile_of(block, corner):
    return block[corner[0] : corner[0] + ROWS, corner[1] : corner[1] + HEAD]


def attend_by_key(bias_ref, query_ref, blocks, out_ref, out_head, key_ref, value_ref):
    is_causal = causal().T

    @pl.when(pl.program_id(0) == 0)
    def _():
        value_ref[HEAD:, :] = jnp.ones((ONES, 5 * ROWS), jnp.bfloat16)

    for at, (block, key_at, value_at) in enumerate(blocks):
        span = slice(at * ROWS, (at + 1) * ROWS)
        key_ref[span, :] = tile_of(block, key_at)
        value_ref[:HEAD, span] = tile_of(block, value_at).T
    queries = jnp.concatenate([query_ref[:, i * HEAD : (i + 1) * HEAD] for i in range(GROUP)], axis=0)
    scores = lax.dot_general(key_ref[...], queries, (((1,), (1,)), ((), ())), preferred_element_type=jnp.float32)
    weights = []
    for i in range(GROUP):
        mine = scores[:, i * ROWS : (i + 1) * ROWS]
        tiles = [jnp.where(is_causal, mine[:ROWS], mine[ROWS : 2 * ROWS]) + bias_ref[0]]
        tiles += [mine[(t + 1) * ROWS : (t + 2) * ROWS] + bias_ref[t] for t in range(1, 4)]
        peak = jnp.maximum(jnp.maximum(tiles[0], tiles[1]), jnp.maximum(tiles[2], tiles[3]))
        peak = jnp.max(peak, axis=0, keepdims=True)
        raised = [jnp.exp2((tile - peak) * EXP2_SCALE) for tile in tiles]
        near = jnp.where(is_causal, raised[0], 0.0).astype(jnp.bfloat16)
        far = jnp.where(is_causal, 0.0, raised[0]).astype(jnp.bfloat16)
        weights.append(jnp.concatenate([near, far] + [r.astype(jnp.bfloat16) for r in raised[1:]], axis=0))
    blended = jnp.dot(value_ref[...], jnp.concatenate(weights, axis=1), preferred_element_type=jnp.float32)
    result = blended[:HEAD] / blended[HEAD : HEAD + 1]
    for i in range(GROUP):
        at = (out_head + i) * HEAD
        out_ref[:, at : at + HEAD] = result[:, i * ROWS : (i + 1) * ROWS].T.astype(jnp.bfloat16)


def attend_by_query(bias_ref, query_ref, blocks, out_ref, out_head, key_ref, value_ref):
    is_causal = causal()

    @pl.when(pl.program_id(0) == 0)
    def _():
        value_ref[:, HEAD:] = jnp.ones((5 * ROWS, HEAD), jnp.bfloat16)

    for at, (block, key_at, value_at) in enumerate(blocks):
        span = slice(at * ROWS, (at + 1) * ROWS)
        key_ref[span, :] = tile_of(block, key_at)
        value_ref[span, :HEAD] = tile_of(block, value_at)

    def some_heads(step, carry):
        spans = [pl.ds(pl.multiple_of((step * PAIR + i) * HEAD, HEAD), HEAD) for i in range(PAIR)]
        queries = jnp.concatenate([query_ref[:, span] for span in spans], axis=0)
        scores = lax.dot_general(
            queries, key_ref[...], (((1,), (1,)), ((), ())), preferred_element_type=jnp.float32
        )
        weights = []
        for i in range(PAIR):
            mine = scores[i * ROWS : (i + 1) * ROWS]
            tiles = [jnp.where(is_causal, mine[:, :ROWS], mine[:, ROWS : 2 * ROWS]) + bias_ref[0]]
            tiles += [mine[:, (t + 1) * ROWS : (t + 2) * ROWS] + bias_ref[t] for t in range(1, 4)]
            peak = jnp.maximum(jnp.maximum(tiles[0], tiles[1]), jnp.maximum(tiles[2], tiles[3]))
            peak = jnp.max(peak, axis=1, keepdims=True)
            raised = [jnp.exp2((tile - peak) * EXP2_SCALE) for tile in tiles]
            near = jnp.where(is_causal, raised[0], 0.0).astype(jnp.bfloat16)
            far = jnp.where(is_causal, 0.0, raised[0]).astype(jnp.bfloat16)
            weights.append(
                jnp.concatenate([near, far] + [r.astype(jnp.bfloat16) for r in raised[1:]], axis=1)
            )
        blended = jnp.dot(
            jnp.concatenate(weights, axis=0), value_ref[...], preferred_element_type=jnp.float32
        )
        result = (blended[:, :HEAD] / blended[:, HEAD:]).astype(jnp.bfloat16)
        for i in range(PAIR):
            span = pl.ds(pl.multiple_of((out_head + step * PAIR + i) * HEAD, HEAD), HEAD)
            out_ref[:, span] = result[i * ROWS : (i + 1) * ROWS]
        return carry

    lax.fori_loop(0, GROUP // PAIR, some_heads, 0, unroll=2)


ONES = 16
BY_QUERY_SCRATCH = [pltpu.VMEM((5 * ROWS, HEAD), jnp.bfloat16), pltpu.VMEM((5 * ROWS, 2 * HEAD), jnp.bfloat16)]
BY_KEY_SCRATCH = [pltpu.VMEM((5 * ROWS, HEAD), jnp.bfloat16), pltpu.VMEM((HEAD + ONES, 5 * ROWS), jnp.bfloat16)]
OUT = pltpu.HBM((1, 2, ROWS, KV * SPAN), jnp.bfloat16)


def block_specs(first):
    whole = pl.BlockSpec((ROWS, 2 * HEAD), lambda i, *p: (0, first + i))
    return [whole, whole, whole, pl.BlockSpec((2 * ROWS, 2 * HEAD), lambda i, *p: (0, i))]


def near_attention(vmem_limit, by_key, half, stride, count, first, bias, queries, blocks, out_shape, out_spec):
    return pl.pallas_call(
        functools.partial(near_attention_kernel, by_key),
        grid=(count,),
        in_specs=[
            pl.BlockSpec((4, ROWS, ROWS), lambda i: (0, 0, 0)),
            pl.BlockSpec((None, None, ROWS, SPAN), lambda i: (0, half, 0, stride * i)),
        ]
        + block_specs(first),
        out_specs=out_spec,
        scratch_shapes=BY_KEY_SCRATCH if by_key else BY_QUERY_SCRATCH,
        out_shape=out_shape,
        compiler_params=pltpu.CompilerParams(vmem_limit_bytes=vmem_limit),
        cost_estimate=pl.CostEstimate(flops=1 << 20, bytes_accessed=1 << 20, transcendentals=0),
        name="near_attention",
    )(bias, queries, *blocks)


def moved_attention(place, queries, blocks, came, into):
    return pl.pallas_call(
        moved_attention_kernel,
        grid_spec=pltpu.PrefetchScalarGridSpec(
            num_scalar_prefetch=1,
            grid=(MOVED,),
            in_specs=[
                pl.BlockSpec((LABEL_ROWS, HEAD), lambda i, p: (LABELS_AT // LABEL_ROWS, 0)),
                pl.BlockSpec((ROWS, SPAN), lambda i, p: (0, i)),
            ]
            + [pl.BlockSpec((2 * ROWS, HEAD), lambda i, p: (i, 0))] * 5
            + [pl.BlockSpec((ROWS, SPAN), lambda i, p: (0, i)), pl.BlockSpec(memory_space=pl.ANY)],
            out_specs=pl.BlockSpec((None, None, ROWS, 2 * SPAN), lambda i, p: (0, 1, 0, i)),
            scratch_shapes=[pltpu.VMEM((4, ROWS, ROWS), jnp.float32)] + BY_KEY_SCRATCH,
        ),
        out_shape=OUT,
        input_output_aliases={9: 0},
        compiler_params=pltpu.CompilerParams(vmem_limit_bytes=SMALL_VMEM_LIMIT),
        cost_estimate=pl.CostEstimate(flops=1 << 20, bytes_accessed=1 << 20, transcendentals=0),
        name="moved_attention",
    )(place, blocks[0], queries, *blocks, came, into)


def shift(block, step, odd_step=None):
    route = [(s, s + (step if odd_step is None or s % 2 == 0 else odd_step)) for s in range(8)]
    return lax.ppermute(block, "seq", [(s, t) for s, t in route if t < 8])


def full_shift(block, targets):
    return lax.ppermute(block, "seq", list(enumerate(targets)))


def other_core(block):
    return lax.ppermute(block, "seq", [(s, s ^ 1) for s in range(8)])


def exchange(block, far, two, low_core, cols):
    pair = jnp.concatenate([two[:, cols], jnp.where(low_core, block[:, cols], far[:, cols])], axis=0)
    return block, far, two, other_core(pair)


def body(hidden, queries, keys, frozen_values, labels, partner, down, up):
    place = lax.axis_index("seq").astype(jnp.int32)
    low_core = lax.rem(place, 2) == 0
    place = place.reshape((1,))
    mask = jnp.bitwise_xor(partner[0], lax.axis_index("dp"))
    near, kv_moved, moved_queries, bias_zero, bias_one = adapter(
        place, labels, hidden, frozen_values, keys, down.T, up, queries
    )
    near_two, near_far = full_shift(near, (2, 3, 4, 5, 6, 7, 0, 1)), full_shift(near, (4, 5, 6, 7, 2, 3, 0, 1))

    def route(m):
        return [(r, r ^ m) for r in range(16)]

    def move(m, kv_moved, moved_queries):
        return lax.ppermute(kv_moved, "dp", route(m)), lax.ppermute(moved_queries, "dp", route(m))

    kv_moved, moved_queries = lax.switch(
        mask - 1, [functools.partial(move, m) for m in range(1, 16)], kv_moved, moved_queries
    )
    kv_moved, moved_queries, near_two, near_far = lax.optimization_barrier(
        (kv_moved, moved_queries, near_two, near_far)
    )
    x = full_shift(kv_moved, (3, 2, 5, 4, 7, 6, 1, 0))
    split = KEPT * 2 * HEAD
    kept_blocks = exchange(near, near_far, near_two, low_core, slice(0, split))
    kept_pair, near_two, near_far = lax.optimization_barrier((kept_blocks[3], near_two, near_far))
    kept_blocks = (near, near_far, near_two, kept_pair)
    zero_blocks = exchange(near, near_far, near_two, low_core, slice(split, None))
    sent = near_attention(
        SMALL_VMEM_LIMIT, True, 1, 2, KEPT, 0, bias_one, queries, kept_blocks,
        jax.ShapeDtypeStruct((ROWS, KEPT * SPAN), jnp.bfloat16), pl.BlockSpec((ROWS, SPAN), lambda i: (0, i)),
    )

    def send(m, sent, kv_moved, bias, queries, *blocks):
        came = lax.ppermute(sent, "dp", route(m))
        two, far, w = shift(kv_moved, 2), shift(kv_moved, 4), shift(kv_moved, 1, 3)
        spec = pl.BlockSpec((None, None, ROWS, SPAN), lambda i: (0, 0, 0, i))
        return came, two, far, w, near_attention(44 << 20, False, 0, 1, KV, KEPT, bias, queries, blocks, OUT, spec)

    came, two, far, w, out = lax.switch(
        mask - 1, [functools.partial(send, m) for m in range(1, 16)], sent, kv_moved, bias_zero, queries, *zero_blocks
    )
    moved_blocks = (kv_moved, far, two, x, w)
    return moved_attention(place, moved_queries, moved_blocks, came, out)


def solution(mesh):
    in_specs = (
        P("dp", None, "seq", None),
        P("dp", None, "seq", None),
        P("dp", None, "seq", None),
        P("dp", None, "seq", None),
        P("dp", None, None),
        P("dp"),
        P(),
        P(),
    )
    out_specs = P("dp", None, "seq", None)
    return jax.shard_map(body, mesh=mesh, in_specs=in_specs, out_specs=out_specs, check_vma=False)
```

```python
import functools

import jax
import jax.numpy as jnp
from jax import lax
from jax.experimental import pallas as pl
from jax.experimental.pallas import tpu as pltpu
from jax.sharding import PartitionSpec as P

HEAD = 128
GROUP = 8
KV = 8
ROWS = 128
SPAN = GROUP * HEAD
PAIR = 2
ADAPTER_SCALE = 2.0
EXP2_SCALE = 1.4426950408889634 / HEAD**0.5
MASKED = -jnp.inf
VMEM_LIMIT = 60 << 20
SMALL_VMEM_LIMIT = 24 << 20

KEPT = KV // 2
MOVED = KV // 2
LABELS_AT = MOVED * 2 * ROWS
LABEL_ROWS = 16


def fill_bias(bias_ref, own_at, places, label_at, by_key):
    def label_row(at):
        found = jnp.where(at >= 0, label_at(jnp.maximum(at, 0)).astype(jnp.float32), -1.0)
        return jnp.broadcast_to(found, (ROWS, ROWS))

    mine = label_row(own_at)
    query_label = mine.T
    merged = jnp.where(causal(), mine, label_row(own_at - 4))
    for at, tile in enumerate([merged] + [label_row(place) for place in places]):
        bias = jnp.where(tile == query_label, 0.0, MASKED)
        bias_ref[at] = bias.T if by_key else bias


def other_places(own_at):
    low_core = lax.rem(own_at, 2) == 0
    return own_at - 2, jnp.where(low_core, own_at - 1, own_at - 3), jnp.where(low_core, own_at - 3, own_at - 1)


def causal():
    rows = lax.broadcasted_iota(jnp.int32, (ROWS, ROWS), 0)
    return lax.broadcasted_iota(jnp.int32, (ROWS, ROWS), 1) <= rows


def adapter_kernel(
    place_ref, labels_ref, hidden_ref, down_ref, frozen_ref, key_ref, up_ref, first_query_ref, second_query_ref,
    near_ref, moved_ref, moved_query_ref, bias_zero_ref, bias_one_ref, low_ref,
):
    step = pl.program_id(0)
    for at, query_ref in enumerate((first_query_ref, second_query_ref)):
        moved_query_ref[:, at * SPAN : (at + 1) * SPAN] = query_ref[...]

    @pl.when(step == 0)
    def _():
        low_ref[...] = jnp.zeros_like(low_ref)
        own_at = place_ref[0]
        for half, bias_ref in enumerate((bias_zero_ref, bias_one_ref)):
            label_at = lambda at: labels_ref[half : half + 1, pl.ds(pl.multiple_of(at * ROWS, ROWS), ROWS)]
            fill_bias(bias_ref, own_at, other_places(own_at), label_at, half == 1)

    low_ref[...] += lax.dot_general(
        hidden_ref[...].reshape(2 * ROWS, hidden_ref.shape[-1]),
        down_ref[...],
        (((1,), (1,)), ((), ())),
        preferred_element_type=jnp.float32,
    )

    def places(half, head):
        if half == 1 and head % 2 == 1:
            at = (head - 1) * ROWS
            return moved_ref.at[at : at + ROWS, :], moved_ref.at[at + ROWS : at + 2 * ROWS, :]
        at = (head if half == 1 else 2 * (KEPT + head)) * HEAD
        return near_ref.at[:, at : at + HEAD], near_ref.at[:, at + HEAD : at + 2 * HEAD]

    for half in range(2):

        @pl.when(step == half)
        def _():
            for head in range(KV):
                cols = slice(head * HEAD, (head + 1) * HEAD)
                key_place, value_place = places(half, head)
                key_place[...] = key_ref[:, cols]
                value_place[...] = frozen_ref[:, cols]

    @pl.when(step == pl.num_programs(0) - 1)
    def _():
        low = low_ref[...].astype(jnp.bfloat16)
        delta = jnp.dot(low, up_ref[...], preferred_element_type=jnp.float32)
        for half in range(2):
            for head in range(KV):
                own = delta[half * ROWS : (half + 1) * ROWS, head * HEAD : (head + 1) * HEAD]
                _, place = places(half, head)
                place[...] = (place[...].astype(jnp.float32) + ADAPTER_SCALE * own).astype(jnp.bfloat16)
        labels = [labels_ref[1:2, at * ROWS : (at + 1) * ROWS].astype(jnp.float32) for at in range(8)]
        labels = jnp.concatenate(labels + [jnp.zeros((LABEL_ROWS - 8, HEAD), jnp.float32)], axis=0)
        moved_ref[LABELS_AT:, :] = labels.astype(jnp.bfloat16)


def adapter(place, labels, hidden, frozen_values, keys, down, up, queries):
    width = hidden.shape[-1]
    steps = MOVED // 2
    part = width // steps
    rank = down.shape[0]
    shapes = [
        ((ROWS, (KEPT + KV) * 2 * HEAD), jnp.bfloat16),
        ((LABELS_AT + LABEL_ROWS, HEAD), jnp.bfloat16),
        ((ROWS, MOVED * SPAN), jnp.bfloat16),
        ((4, ROWS, ROWS), jnp.float32),
        ((4, ROWS, ROWS), jnp.float32),
    ]
    return pl.pallas_call(
        adapter_kernel,
        grid_spec=pltpu.PrefetchScalarGridSpec(
            num_scalar_prefetch=1,
            grid=(steps,),
            in_specs=[
                pl.BlockSpec((None, 2, 8 * ROWS), lambda i, p: (0, 0, 0)),
                pl.BlockSpec((None, 2, ROWS, part), lambda i, p: (0, 0, 0, i)),
                pl.BlockSpec((rank, part), lambda i, p: (0, i)),
                pl.BlockSpec((None, None, ROWS, KV * HEAD), lambda i, p: (0, i, 0, 0)),
                pl.BlockSpec((None, None, ROWS, KV * HEAD), lambda i, p: (0, i, 0, 0)),
                pl.BlockSpec((rank, KV * HEAD), lambda i, p: (0, 0)),
                pl.BlockSpec((None, None, ROWS, SPAN), lambda i, p: (0, 1, 0, 4 * i + 1)),
                pl.BlockSpec((None, None, ROWS, SPAN), lambda i, p: (0, 1, 0, 4 * i + 3)),
            ],
            out_specs=[
                pl.BlockSpec((ROWS, 2 * SPAN), lambda i, p: (0, i))
                if at == 2
                else pl.BlockSpec(shape, lambda i, p, n=len(shape): (0,) * n)
                for at, (shape, _) in enumerate(shapes)
            ],
            scratch_shapes=[pltpu.VMEM((2 * ROWS, rank), jnp.float32)],
        ),
        out_shape=[jax.ShapeDtypeStruct(*shape) for shape in shapes],
        compiler_params=pltpu.CompilerParams(vmem_limit_bytes=60 << 20),
        cost_estimate=pl.CostEstimate(flops=1 << 20, bytes_accessed=1 << 20, transcendentals=0),
        name="adapter",
    )(place, labels, hidden, down, frozen_values, keys, up, queries, queries)


def near_attention_kernel(by_key, bias_ref, query_ref, own_ref, far_ref, two_ref, pair_ref, out_ref, key_ref, value_ref):
    blocks = [(block, (at, 0), (at, HEAD)) for block, at in ((own_ref, 0), (far_ref, 0), (two_ref, 0), (pair_ref, 0), (pair_ref, ROWS))]
    attend = attend_by_key if by_key else attend_by_query
    attend(bias_ref, query_ref, blocks, out_ref, 0, key_ref, value_ref)


def moved_attention_kernel(
    place_ref, label_ref, query_ref, own_ref, far_ref, two_ref, x_ref, w_ref, came_ref, _,
    out_ref, bias_ref, key_ref, value_ref,
):
    @pl.when(pl.program_id(0) == 0)
    def _():
        own_at = place_ref[0]
        rows = label_ref[...].astype(jnp.float32)
        chosen = lax.broadcasted_iota(jnp.int32, rows.shape, 0)

        def label_at(at):
            return jnp.sum(jnp.where(chosen == at, rows, 0.0), axis=0, keepdims=True)

        fill_bias(bias_ref, own_at, other_places(own_at), label_at, True)

    out_ref[:, :SPAN] = came_ref[...]
    blocks = [(block, (0, 0), (ROWS, 0)) for block in (own_ref, far_ref, two_ref, x_ref, w_ref)]
    attend_by_key(bias_ref, query_ref, blocks, out_ref, GROUP, key_ref, value_ref)


def tile_of(block, corner):
    return block[corner[0] : corner[0] + ROWS, corner[1] : corner[1] + HEAD]


def attend_by_key(bias_ref, query_ref, blocks, out_ref, out_head, key_ref, value_ref):
    is_causal = causal().T

    @pl.when(pl.program_id(0) == 0)
    def _():
        value_ref[HEAD:, :] = jnp.ones((ONES, 5 * ROWS), jnp.bfloat16)

    for at, (block, key_at, value_at) in enumerate(blocks):
        span = slice(at * ROWS, (at + 1) * ROWS)
        key_ref[span, :] = tile_of(block, key_at)
        value_ref[:HEAD, span] = tile_of(block, value_at).T
    queries = jnp.concatenate([query_ref[:, i * HEAD : (i + 1) * HEAD] for i in range(GROUP)], axis=0)
    scores = lax.dot_general(key_ref[...], queries, (((1,), (1,)), ((), ())), preferred_element_type=jnp.float32)
    weights = []
    for i in range(GROUP):
        mine = scores[:, i * ROWS : (i + 1) * ROWS]
        tiles = [jnp.where(is_causal, mine[:ROWS], mine[ROWS : 2 * ROWS]) + bias_ref[0]]
        tiles += [mine[(t + 1) * ROWS : (t + 2) * ROWS] + bias_ref[t] for t in range(1, 4)]
        peak = jnp.maximum(jnp.maximum(tiles[0], tiles[1]), jnp.maximum(tiles[2], tiles[3]))
        peak = jnp.max(peak, axis=0, keepdims=True)
        raised = [jnp.exp2((tile - peak) * EXP2_SCALE) for tile in tiles]
        near = jnp.where(is_causal, raised[0], 0.0).astype(jnp.bfloat16)
        far = jnp.where(is_causal, 0.0, raised[0]).astype(jnp.bfloat16)
        weights.append(jnp.concatenate([near, far] + [r.astype(jnp.bfloat16) for r in raised[1:]], axis=0))
    blended = jnp.dot(value_ref[...], jnp.concatenate(weights, axis=1), preferred_element_type=jnp.float32)
    result = blended[:HEAD] / blended[HEAD : HEAD + 1]
    for i in range(GROUP):
        at = (out_head + i) * HEAD
        out_ref[:, at : at + HEAD] = result[:, i * ROWS : (i + 1) * ROWS].T.astype(jnp.bfloat16)


def attend_by_query(bias_ref, query_ref, blocks, out_ref, out_head, key_ref, value_ref):
    is_causal = causal()

    @pl.when(pl.program_id(0) == 0)
    def _():
        value_ref[:, HEAD:] = jnp.ones((5 * ROWS, HEAD), jnp.bfloat16)

    for at, (block, key_at, value_at) in enumerate(blocks):
        span = slice(at * ROWS, (at + 1) * ROWS)
        key_ref[span, :] = tile_of(block, key_at)
        value_ref[span, :HEAD] = tile_of(block, value_at)

    def some_heads(step, carry):
        spans = [pl.ds(pl.multiple_of((step * PAIR + i) * HEAD, HEAD), HEAD) for i in range(PAIR)]
        queries = jnp.concatenate([query_ref[:, span] for span in spans], axis=0)
        scores = lax.dot_general(
            queries, key_ref[...], (((1,), (1,)), ((), ())), preferred_element_type=jnp.float32
        )
        weights = []
        for i in range(PAIR):
            mine = scores[i * ROWS : (i + 1) * ROWS]
            tiles = [jnp.where(is_causal, mine[:, :ROWS], mine[:, ROWS : 2 * ROWS]) + bias_ref[0]]
            tiles += [mine[:, (t + 1) * ROWS : (t + 2) * ROWS] + bias_ref[t] for t in range(1, 4)]
            peak = jnp.maximum(jnp.maximum(tiles[0], tiles[1]), jnp.maximum(tiles[2], tiles[3]))
            peak = jnp.max(peak, axis=1, keepdims=True)
            raised = [jnp.exp2((tile - peak) * EXP2_SCALE) for tile in tiles]
            near = jnp.where(is_causal, raised[0], 0.0).astype(jnp.bfloat16)
            far = jnp.where(is_causal, 0.0, raised[0]).astype(jnp.bfloat16)
            weights.append(
                jnp.concatenate([near, far] + [r.astype(jnp.bfloat16) for r in raised[1:]], axis=1)
            )
        blended = jnp.dot(
            jnp.concatenate(weights, axis=0), value_ref[...], preferred_element_type=jnp.float32
        )
        result = (blended[:, :HEAD] / blended[:, HEAD:]).astype(jnp.bfloat16)
        for i in range(PAIR):
            span = pl.ds(pl.multiple_of((out_head + step * PAIR + i) * HEAD, HEAD), HEAD)
            out_ref[:, span] = result[i * ROWS : (i + 1) * ROWS]
        return carry

    lax.fori_loop(0, GROUP // PAIR, some_heads, 0, unroll=2)


ONES = 16
BY_QUERY_SCRATCH = [pltpu.VMEM((5 * ROWS, HEAD), jnp.bfloat16), pltpu.VMEM((5 * ROWS, 2 * HEAD), jnp.bfloat16)]
BY_KEY_SCRATCH = [pltpu.VMEM((5 * ROWS, HEAD), jnp.bfloat16), pltpu.VMEM((HEAD + ONES, 5 * ROWS), jnp.bfloat16)]
OUT = pltpu.HBM((1, 2, ROWS, KV * SPAN), jnp.bfloat16)


def block_specs(first):
    whole = pl.BlockSpec((ROWS, 2 * HEAD), lambda i, *p: (0, first + i))
    return [whole, whole, whole, pl.BlockSpec((2 * ROWS, 2 * HEAD), lambda i, *p: (0, i))]


def near_attention(vmem_limit, by_key, half, stride, count, first, bias, queries, blocks, out_shape, out_spec):
    return pl.pallas_call(
        functools.partial(near_attention_kernel, by_key),
        grid=(count,),
        in_specs=[
            pl.BlockSpec((4, ROWS, ROWS), lambda i: (0, 0, 0)),
            pl.BlockSpec((None, None, ROWS, SPAN), lambda i: (0, half, 0, stride * i)),
        ]
        + block_specs(first),
        out_specs=out_spec,
        scratch_shapes=BY_KEY_SCRATCH if by_key else BY_QUERY_SCRATCH,
        out_shape=out_shape,
        compiler_params=pltpu.CompilerParams(vmem_limit_bytes=vmem_limit),
        cost_estimate=pl.CostEstimate(flops=1 << 20, bytes_accessed=1 << 20, transcendentals=0),
        name="near_attention",
    )(bias, queries, *blocks)


def moved_attention(place, queries, blocks, came, into):
    return pl.pallas_call(
        moved_attention_kernel,
        grid_spec=pltpu.PrefetchScalarGridSpec(
            num_scalar_prefetch=1,
            grid=(MOVED,),
            in_specs=[
                pl.BlockSpec((LABEL_ROWS, HEAD), lambda i, p: (LABELS_AT // LABEL_ROWS, 0)),
                pl.BlockSpec((ROWS, SPAN), lambda i, p: (0, i)),
            ]
            + [pl.BlockSpec((2 * ROWS, HEAD), lambda i, p: (i, 0))] * 5
            + [pl.BlockSpec((ROWS, SPAN), lambda i, p: (0, i)), pl.BlockSpec(memory_space=pl.ANY)],
            out_specs=pl.BlockSpec((None, None, ROWS, 2 * SPAN), lambda i, p: (0, 1, 0, i)),
            scratch_shapes=[pltpu.VMEM((4, ROWS, ROWS), jnp.float32)] + BY_KEY_SCRATCH,
        ),
        out_shape=OUT,
        input_output_aliases={9: 0},
        compiler_params=pltpu.CompilerParams(vmem_limit_bytes=SMALL_VMEM_LIMIT),
        cost_estimate=pl.CostEstimate(flops=1 << 20, bytes_accessed=1 << 20, transcendentals=0),
        name="moved_attention",
    )(place, blocks[0], queries, *blocks, came, into)


def shift(block, step, odd_step=None):
    route = [(s, s + (step if odd_step is None or s % 2 == 0 else odd_step)) for s in range(8)]
    return lax.ppermute(block, "seq", [(s, t) for s, t in route if t < 8])


def full_shift(block, targets):
    return lax.ppermute(block, "seq", list(enumerate(targets)))


def other_core(block):
    return lax.ppermute(block, "seq", [(s, s ^ 1) for s in range(8)])


def exchange(block, far, two, low_core, cols):
    pair = jnp.concatenate([two[:, cols], jnp.where(low_core, block[:, cols], far[:, cols])], axis=0)
    return block, far, two, other_core(pair)


def body(hidden, queries, keys, frozen_values, labels, partner, down, up):
    place = lax.axis_index("seq").astype(jnp.int32)
    low_core = lax.rem(place, 2) == 0
    place = place.reshape((1,))
    mask = jnp.bitwise_xor(partner[0], lax.axis_index("dp"))
    near, kv_moved, moved_queries, bias_zero, bias_one = adapter(
        place, labels, hidden, frozen_values, keys, down.T, up, queries
    )
    near_two, near_far = full_shift(near, (2, 3, 4, 5, 6, 7, 0, 1)), full_shift(near, (4, 5, 6, 7, 2, 3, 0, 1))

    def route(m):
        return [(r, r ^ m) for r in range(16)]

    def move(m, kv_moved, moved_queries):
        return lax.ppermute(kv_moved, "dp", route(m)), lax.ppermute(moved_queries, "dp", route(m))

    kv_moved, moved_queries = lax.switch(
        mask - 1, [functools.partial(move, m) for m in range(1, 16)], kv_moved, moved_queries
    )
    kv_moved, moved_queries, near_two, near_far = lax.optimization_barrier(
        (kv_moved, moved_queries, near_two, near_far)
    )
    x = full_shift(kv_moved, (3, 2, 5, 4, 7, 6, 1, 0))
    split = KEPT * 2 * HEAD
    kept_blocks = exchange(near, near_far, near_two, low_core, slice(0, split))
    kept_pair, near_two, near_far = lax.optimization_barrier((kept_blocks[3], near_two, near_far))
    kept_blocks = (near, near_far, near_two, kept_pair)
    zero_blocks = exchange(near, near_far, near_two, low_core, slice(split, None))
    sent = near_attention(
        SMALL_VMEM_LIMIT, True, 1, 2, KEPT, 0, bias_one, queries, kept_blocks,
        jax.ShapeDtypeStruct((ROWS, KEPT * SPAN), jnp.bfloat16), pl.BlockSpec((ROWS, SPAN), lambda i: (0, i)),
    )

    def send(m, sent, kv_moved, bias, queries, *blocks):
        came = lax.ppermute(sent, "dp", route(m))
        two, far, w = shift(kv_moved, 2), shift(kv_moved, 4), shift(kv_moved, 1, 3)
        spec = pl.BlockSpec((None, None, ROWS, SPAN), lambda i: (0, 0, 0, i))
        return came, two, far, w, near_attention(44 << 20, False, 0, 1, KV, KEPT, bias, queries, blocks, OUT, spec)

    came, two, far, w, out = lax.switch(
        mask - 1, [functools.partial(send, m) for m in range(1, 16)], sent, kv_moved, bias_zero, queries, *zero_blocks
    )
    moved_blocks = (kv_moved, far, two, x, w)
    return moved_attention(place, moved_queries, moved_blocks, came, out)


def solution(mesh):
    in_specs = (
        P("dp", None, "seq", None),
        P("dp", None, "seq", None),
        P("dp", None, "seq", None),
        P("dp", None, "seq", None),
        P("dp", None, None),
        P("dp"),
        P(),
        P(),
    )
    out_specs = P("dp", None, "seq", None)
    return jax.shard_map(body, mesh=mesh, in_specs=in_specs, out_specs=out_specs, check_vma=False)
```
